256 devices in a mesh: group: 8 (over x, core), dev: 32 (over z, y).
Axes of the slice: x: 4, y: 4, z: 8, core: 2. Of those that a mesh axis runs over, the one named last changes fastest.
Arguments:
- charges: float32 [64, 1048576], P(None, ('group', 'dev')), may hold values from -6 to 6
- coords: float32 [3, 1048576], P(None, ('group', 'dev')), may hold values from 0 to 1
- point_order: int32 [256, 4096], P(('group', 'dev')), may hold values from 0 to 4095, each once within a row
- near_list: int32 [8192, 27], P(('group', 'dev')), may hold values from 0 to 47
- send_list: int32 [256, 256], P(('group', 'dev')), may hold values from 0 to 31
- recv_list: int32 [256, 256], P(('group', 'dev')), may hold values from 0 to 255, each once within a row
- leaf_basis: float32 [32, 1048576], P(None, ('group', 'dev')), may hold values from -0.5 to 0.5
- local_transfer: float32 [15872, 1024], P(('group', 'dev')), may hold values from -0.75 to 0.75
- leaf_coupling: float32 [65536, 1024], P(('group', 'dev')), may hold values from -0.375 to 0.375
- group_transfer: float32 [496, 1024], P('group'), may hold values from -0.75 to 0.75
- top_coupling: float32 [8, 32, 256], P('group'), may hold values from -0.375 to 0.375
Outputs:
- potential: float32 [64, 1048576], P(None, ('group', 'dev'))
The draws below stay inside these ranges and needn't reach their ends.
Inputs may be any that keep to these rules, and one draw needn't show every extreme that they name: `point_order`: each row is a permutation of 0 to 4095. `recv_list`: each row is a permutation of 0 to 255.
All inputs are finite; a program needn't handle non-finite values.
Results may differ from the reference program's by a relative error of at most 0.0003.
Values sent between devices are 32-bit elements; how exact they have to be, the bound alone decides.
No kernel may reach another device: no remote copies, remote signals or barrier semaphores. Data moves between devices by JAX's collectives and lax.ppermute only.
A program may use at most 64 MiB of HBM per device.

```python
import jax
import jax.numpy as jnp
from jax import lax

LEAF = 128
RANK = 32
RHS = 64
NEAR = 27
INTER = 8
HALO_L = 8
LEAF_DEV = 32
PTS_DEV = 4096
LEAVES = 8192
NPTS = 1048576
SLOTS_DEV = 256
SLOT = 8
WIN = 48
N_GROUP = 8
N_DEV = 32
DEVICES = 256


def with_ends(values, own_key, smallest, high):
    longest = values.shape.index(max(values.shape))
    spots = []
    for shift in (0, 1):
        where = [jax.random.randint(jax.random.fold_in(own_key, axis), (), 0, length) for axis, length in enumerate(values.shape)]
        where[longest] = (where[longest] + shift) % values.shape[longest]
        spots.append(tuple(where))
    return values.at[spots[0]].set(smallest).at[spots[1]].set(high)


def levels(rng, shape, shards, low, high):
    def one(position, shards_of):
        steps = jax.random.uniform(jax.random.fold_in(jax.random.fold_in(rng, 6), position), (shards_of,), jnp.float32, low / len(shards), high / len(shards))
        return jnp.repeat(jnp.exp(steps), shape[position] // shards_of).reshape((-1,) + (1,) * (len(shape) - position - 1))

    loudness = one(*shards[0])
    for cut in shards[1:]:
        loudness = loudness * one(*cut)
    return loudness


def scatter_about(key, shape, deviation, most, cuts=(), kind=jnp.bfloat16):
    entries = jax.random.normal(key, shape, jnp.float32) * deviation
    if len(cuts) > 0:
        entries = levels(key, shape, cuts, -0.22, 0.18) * entries
    return jnp.clip(entries, min=-most, max=most).astype(kind)


def setup_inputs(seed: int = 0) -> dict:
    streams_of = jax.random.split(jax.random.key(seed), 12)
    return {
        "charges": scatter_about(streams_of[0], (RHS, NPTS), 1.0, 6.0, ((1, 256),), jnp.float32),
        "coords": jnp.clip(1.0 * jax.random.uniform(streams_of[1], (3, NPTS), jnp.float32) ** levels(streams_of[1], (3, NPTS), ((1, 256),), -0.2, 0.2), 0.0, 1.0),
        "point_order": jax.vmap(lambda own: jax.random.permutation(own, PTS_DEV))(jax.random.split(streams_of[2], DEVICES)).reshape((DEVICES, PTS_DEV)).astype(jnp.int32),
        "near_list": with_ends(jax.random.randint(streams_of[3], (LEAVES, NEAR), 0, WIN), jax.random.fold_in(streams_of[3], 1), 0, WIN - 1).astype(jnp.int32),
        "send_list": with_ends(jax.random.randint(streams_of[4], (DEVICES, SLOTS_DEV), 0, LEAF_DEV), jax.random.fold_in(streams_of[4], 1), 0, LEAF_DEV - 1).astype(jnp.int32),
        "recv_list": jax.vmap(lambda own: jax.random.permutation(own, SLOTS_DEV))(jax.random.split(streams_of[5], DEVICES)).reshape((DEVICES, SLOTS_DEV)).astype(jnp.int32),
        "leaf_basis": scatter_about(streams_of[6], (RANK, NPTS), LEAF ** -0.5, 0.5, ((1, 256),), jnp.float32),
        "local_transfer": scatter_about(streams_of[7], (DEVICES * (2 * LEAF_DEV - 2), RANK * RANK), (2 * RANK) ** -0.5, 0.75, ((0, 256),), jnp.float32),
        "leaf_coupling": scatter_about(streams_of[8], (LEAVES * INTER, RANK * RANK), (INTER * RANK) ** -0.5, 0.375, ((0, 256),), jnp.float32),
        "group_transfer": scatter_about(streams_of[9], (N_GROUP * (2 * N_DEV - 2), RANK * RANK), (2 * RANK) ** -0.5, 0.75, ((0, 8),), jnp.float32),
        "top_coupling": scatter_about(streams_of[10], (N_GROUP, RANK, N_GROUP * RANK), (N_GROUP * RANK) ** -0.5, 0.375, ((0, 8),), jnp.float32),
    }


signal_var = 0.1
length_scale = 0.3
smoothing = 1e-06
down_gain = 2.0 ** 0.5
highest = lax.Precision.HIGHEST

def matern(squared):
    radius = jnp.sqrt(squared + smoothing)
    scaled = 3.0 ** 0.5 / length_scale * radius
    return signal_var * (1.0 + scaled) * jnp.exp(-scaled)

def near_block(targets, sources):
    columns = targets.shape[0] - 3
    squared = jnp.zeros(sources.shape[1:3] + (targets.shape[2], sources.shape[3]), jnp.float32)
    for component in range(3):
        difference = targets[columns + component][:, None, :, None] - sources[columns + component][:, :, None, :]
        squared = squared + difference * difference
    kernel = matern(squared)
    return jnp.einsum('cjpq,kcjq->kcp', kernel, sources[:columns], precision=highest)

def climb(tree_nodes, transfer):
    rank_size = tree_nodes.shape[-2]
    offset = 0
    while tree_nodes.shape[-3] > 1:
        level_count = tree_nodes.shape[-3]
        matrices = transfer[..., offset:offset + level_count, :].reshape(transfer.shape[:-2] + (level_count, rank_size, rank_size))
        carried = jnp.einsum('...crs,...csk->...crk', matrices, tree_nodes, precision=highest)
        tree_nodes = carried[..., 0::2, :, :] + carried[..., 1::2, :, :]
        offset = offset + level_count
    return tree_nodes[..., 0, :, :]

def descend(top_value, transfer, leaf_count):
    rank_size = top_value.shape[-2]
    tree_nodes = top_value[..., None, :, :]
    span_width = 1
    while span_width < leaf_count:
        span_width = span_width * 2
        offset = 2 * leaf_count - 2 * span_width
        matrices = transfer[..., offset:offset + span_width, :].reshape(transfer.shape[:-2] + (span_width, rank_size, rank_size))
        parents = jnp.repeat(tree_nodes, 2, axis=-3)
        tree_nodes = down_gain * jnp.einsum('...csr,...csk->...crk', matrices, parents, precision=highest)
    return tree_nodes

def reference(charges, coords, point_order, near_list, send_list, recv_list, leaf_basis, local_transfer, leaf_coupling, group_transfer, top_coupling):
    columns = charges.shape[0]
    rank_size = leaf_basis.shape[0]
    per_device = LEAF_DEV * LEAF
    device_total = N_GROUP * N_DEV
    stacked = jnp.concatenate([charges, coords], 0).reshape(columns + 3, device_total, per_device)
    stacked = jax.vmap(lambda block_rows, ordering: block_rows[:, ordering], in_axes=(1, 0), out_axes=1)(stacked, point_order)
    values = stacked[:columns].reshape(columns, device_total, LEAF_DEV, LEAF)
    leaf_bases = leaf_basis.reshape(rank_size, device_total, LEAF_DEV, LEAF)
    coefficients = jnp.einsum('rdlp,kdlp->dlrk', leaf_bases, values, precision=highest)
    local_mats = local_transfer.reshape(device_total, 2 * LEAF_DEV - 2, rank_size * rank_size)
    block_root = climb(coefficients, local_mats)
    group_mats = group_transfer.reshape(N_GROUP, 2 * N_DEV - 2, rank_size * rank_size)
    group_root = climb(block_root.reshape(N_GROUP, N_DEV, rank_size, columns), group_mats)
    top_local = jnp.einsum('grh,hk->grk', top_coupling, group_root.reshape(N_GROUP * rank_size, columns), precision=highest)
    block_local = descend(top_local, group_mats, N_DEV).reshape(device_total, rank_size, columns)
    leaf_down = descend(block_local, local_mats, LEAF_DEV)
    leaf_rows = coefficients.reshape(device_total * LEAF_DEV, rank_size * columns)
    slot_owner = jnp.arange(SLOTS_DEV, dtype=jnp.int32) // SLOT
    slot_within = jnp.arange(SLOTS_DEV, dtype=jnp.int32) % SLOT
    couplings = leaf_coupling.reshape(device_total, SLOTS_DEV, rank_size, rank_size)

    def far_leaves(device_index):
        group_index = device_index // N_DEV
        place_index = device_index % N_DEV
        source_device = group_index * N_DEV + slot_owner
        sent_leaves = send_list[source_device, place_index * SLOT + slot_within]
        received = leaf_rows[source_device * LEAF_DEV + sent_leaves]
        picked = received[recv_list[device_index]].reshape(SLOTS_DEV, rank_size, columns)
        products = jnp.einsum('nrs,nsk->nrk', couplings[device_index], picked, precision=highest)
        return products.reshape(LEAF_DEV, INTER, rank_size, columns).sum(1)
    leaf_far = lax.map(far_leaves, jnp.arange(device_total, dtype=jnp.int32))
    total_local = leaf_down + leaf_far
    far_field = jnp.einsum('rdlp,dlrk->kdlp', leaf_bases, total_local, precision=highest).reshape(columns, device_total * per_device)
    halo_width = HALO_L * LEAF
    padded = jnp.pad(stacked.reshape(columns + 3, device_total * per_device), ((0, 0), (halo_width, halo_width)))
    near_rows = near_list.reshape(device_total, LEAF_DEV, NEAR)

    def near_device(device_index):
        start = (device_index * per_device).astype(jnp.int32)
        window = lax.dynamic_slice_in_dim(padded, start, per_device + 2 * halo_width, 1).reshape(columns + 3, LEAF_DEV + 2 * HALO_L, LEAF)
        targets = window[:, HALO_L:HALO_L + LEAF_DEV]
        sources = window[:, near_rows[device_index]]
        return near_block(targets, sources)
    near_parts = lax.map(near_device, jnp.arange(device_total, dtype=jnp.int32))
    near_field = jnp.transpose(near_parts, (1, 0, 2, 3)).reshape(columns, device_total * per_device)
    return near_field + far_field
```

```python
import functools

import jax
import jax.numpy as jnp
from jax import lax
from jax.experimental import pallas as pl
from jax.experimental.pallas import tpu as pltpu
from jax.sharding import PartitionSpec as P

f32 = jnp.float32
bf16 = jnp.bfloat16
highest = lax.Precision.HIGHEST

LEAF = 128
RANK = 32
RHS = 64
LEAVES = 32
PTS = 4096
NEAR = 27
CHUNK = 14
HALO_L = 8
HALO = HALO_L * LEAF
WIN_L = LEAVES + 2 * HALO_L
WIN = WIN_L * LEAF
INTER = 8
GROUPS = 8
MEMBERS = 32
PACK = HALO // 2 + 8 * HALO_L
FEATURES = 48

LOG2E = 1.4426950408889634
SCALE = LOG2E * 3.0**0.5 / 0.3
FLOOR = SCALE * SCALE * 1e-6
WEIGHT = 0.1 / LOG2E
DOWN = 2.0**0.5
VMEM_BYTES = 48 * 1024 * 1024

vmem = pl.BlockSpec(memory_space=pltpu.VMEM)
smem = pl.BlockSpec(memory_space=pltpu.SMEM)


def block(index, size):
    return pl.ds(pl.multiple_of(index * size, size), size)


def dot(a, b):
    return jnp.dot(a, b, precision=highest, preferred_element_type=f32)


def left_half(shape):
    return lax.broadcasted_iota(jnp.int32, shape, len(shape) - 1) < RHS


def swap(x):
    return pltpu.roll(x, RHS, 1)


def both(x):
    return jnp.where(left_half(x.shape), x, swap(x))


def fold(x):
    half = RANK // 2
    return jnp.where(left_half((half, 2 * RHS)), x[:half], swap(x[half:]))


def unfold(x):
    return jnp.concatenate([x, swap(x)], axis=0)


def two(x):
    high = x.astype(bf16)
    return high, (x - high.astype(f32)).astype(bf16)


def three(x):
    high = x.astype(bf16).astype(f32)
    rest = x - high
    middle = rest.astype(bf16).astype(f32)
    return high, middle, rest - middle


def order_kernel(
    order_ref, send_ref, charges_ref, coords_ref, basis_ref,
    rows_ref, places_ref, first_ref, last_ref, coef_ref, sent_ref,
    turned_ref, padded_ref,
):
    padded_ref[...] = jnp.zeros_like(padded_ref)
    padded_ref[0:3, :] = coords_ref[...]

    def turn(b, carry):
        columns = block(b, LEAF)
        tall = jnp.concatenate(
            [charges_ref[:, columns], padded_ref[:, columns], jnp.zeros((56, LEAF), f32)], axis=0
        )
        turned_ref[columns, :] = tall.T
        return carry

    lax.fori_loop(0, LEAVES, turn, 0)

    def fetch(b, carry):
        for i in range(32):
            at = b * 32 + i
            rows_ref[pl.ds(at, 1), :] = turned_ref[pl.ds(order_ref[0, at], 1), :]
        return carry

    lax.fori_loop(0, PTS // 32, fetch, 0)

    def coefficient(l, carry):
        columns = block(l, LEAF)
        rows = rows_ref[columns, :]
        coef_ref[l] = both(dot(basis_ref[:, columns], rows))
        places_ref[:, columns] = rows.T[RHS : RHS + 8]
        return carry

    lax.fori_loop(0, LEAVES, coefficient, 0)

    for ref, start in ((first_ref, 0), (last_ref, PTS - HALO)):
        near = rows_ref[start : start + HALO // 2, :]
        far = rows_ref[start + HALO // 2 : start + HALO, :]
        ref[: HALO // 2, :] = jnp.where(left_half(near.shape), near, swap(far))
        for i in range(HALO_L):
            ref[HALO // 2 + 8 * i : HALO // 2 + 8 * i + 8, :] = places_ref[
                :, start + i * LEAF : start + (i + 1) * LEAF
            ]

    left = left_half((RANK, 2 * RHS))

    def pack(d, carry):
        for q in range(4):
            one = coef_ref[send_ref[0, d * 8 + 2 * q]]
            other = coef_ref[send_ref[0, d * 8 + 2 * q + 1]]
            sent_ref[d, q * RANK : (q + 1) * RANK, :] = jnp.where(left, one, other)
        return carry

    lax.fori_loop(0, MEMBERS, pack, 0)


def near_kernel(
    list_ref, bias_ref, rows_ref, places_ref, before_ref, after_ref,
    out_ref, target_ref, source_ref, weight_ref,
):
    row = lax.broadcasted_iota(jnp.int32, (8, LEAF), 0)
    zero = jnp.zeros((8, LEAF), f32)

    def features(w, places):
        c = jnp.where(row < 3, (places - 0.5) * SCALE, 0.0)
        squares = jnp.sum(c * c, axis=0, keepdims=True) + 0.5 * FLOOR
        parts = three(jnp.broadcast_to(squares, (8, LEAF)))
        h, m, l = three(c)
        norm = jnp.where(row == 3, parts[0], jnp.where(row == 4, parts[1], parts[2]))
        is_norm = jnp.logical_and(row >= 3, row < 6)
        norm = jnp.where(is_norm, norm, 0.0)
        ones = jnp.where(is_norm, 1.0, 0.0)
        columns = block(w, LEAF)
        source = jnp.concatenate([h + ones, m + norm, l, h, m, h], axis=0)
        source_ref[:, columns] = source.astype(bf16)
        target = jnp.concatenate(
            [-2.0 * h + norm, -2.0 * h + ones, -2.0 * h, -2.0 * m, -2.0 * m, -2.0 * l], axis=0
        )
        return target

    def weigh(w, x):
        scaled = x * WEIGHT
        high = scaled.astype(bf16).astype(f32)
        low = scaled - high
        both_parts = jnp.where(left_half(x.shape), high, swap(low))
        weight_ref[block(w, LEAF), :] = both_parts.astype(bf16)

    def own(b, carry):
        columns = block(b, LEAF)
        target = features(b + HALO_L, places_ref[:, columns])
        target = jnp.concatenate([target] + [zero] * 10, axis=0)
        target_ref[columns, :] = target.T[:, :FEATURES].astype(bf16)
        weigh(b + HALO_L, rows_ref[columns, :])
        return carry

    lax.fori_loop(0, LEAVES, own, 0)
    for ref, start in ((before_ref, 0), (after_ref, HALO_L + LEAVES)):
        for i in range(HALO_L):
            features(start + i, ref[HALO // 2 + 8 * i : HALO // 2 + 8 * i + 8, :])
            x = ref[(i % 4) * LEAF : (i % 4 + 1) * LEAF, :]
            weigh(start + i, x if i < 4 else swap(x))

    def leaf(a, carry):
        target = target_ref[block(a, LEAF), :]
        total = jnp.zeros((LEAF, 2 * RHS), f32)
        for j in range(0, NEAR + 1, CHUNK):
            at = [block(list_ref[a, j + i], LEAF) for i in range(CHUNK)]
            source = jnp.concatenate([source_ref[:, s] for s in at], axis=1)
            weight = jnp.concatenate([weight_ref[s, :] for s in at], axis=0)
            squared = jnp.dot(target, source, preferred_element_type=f32)
            parts = []
            for i in range(CHUNK):
                r = jnp.maximum(squared[:, i * LEAF : (i + 1) * LEAF], FLOOR)
                t = r * lax.rsqrt(r)
                parts.append((t + LOG2E) * jnp.exp2(bias_ref[a, j + i] - t))
            high, low = two(jnp.concatenate(parts, axis=1))
            first = jnp.dot(high, weight, preferred_element_type=f32)
            second = jnp.dot(low, weight, preferred_element_type=f32)
            total = total + (first + swap(first) + second)
        out_ref[:, block(a, LEAF)] = total.T[:RHS]
        return carry

    lax.fori_loop(0, LEAVES, leaf, 0)


def up_kernel(place_ref, coef_ref, pair_ref, path_ref, out_ref, level_ref):
    level_ref[...] = coef_ref[...].reshape(level_ref.shape)
    offset, count = 0, LEAVES
    while count > 1:
        values = [
            dot(pair_ref[offset + i], level_ref[2 * RANK * i : 2 * RANK * (i + 1), :])
            for i in range(count // 2)
        ]
        for i, value in enumerate(values):
            level_ref[RANK * i : RANK * (i + 1), :] = value
        offset, count = offset + count // 2, count // 2
    value = level_ref[:RANK, :]
    position = place_ref[0]
    offset, count = 0, MEMBERS
    while count > 1:
        value = dot(path_ref[offset + position], value)
        offset, count, position = offset + count, count // 2, lax.shift_right_logical(position, 1)
    packed = fold(value)
    for g in range(GROUPS):
        out_ref[g] = packed


def top_kernel(roots_ref, coupling_ref, out_ref):
    stacked = jnp.concatenate([unfold(roots_ref[g]) for g in range(GROUPS)], axis=0)
    packed = fold(dot(coupling_ref[0], stacked))
    for d in range(MEMBERS):
        out_ref[d] = packed


def final_kernel(
    place_ref, recv_ref, tops_ref, path_ref, pair_ref, slots_ref, coupling_ref, basis_ref, near_ref,
    out_ref, level_ref,
):
    folded = tops_ref[0]
    for d in range(1, MEMBERS):
        folded = folded + tops_ref[d]
    value = both(unfold(folded))
    position = place_ref[0]
    offset, count = 2 * MEMBERS - 4, 2
    while count <= MEMBERS:
        child = position // (MEMBERS // count)
        value = DOWN * dot(path_ref[offset + child], value)
        count = count * 2
        offset = offset - count
    nodes = [value]
    offset = LEAVES - 2
    while len(nodes) < LEAVES:
        children = [DOWN * dot(pair_ref[offset + i], node) for i, node in enumerate(nodes)]
        nodes = [c[RANK * k : RANK * (k + 1)] for c in children for k in (0, 1)]
        offset = offset - len(nodes)
    for i, node in enumerate(nodes):
        level_ref[i] = node

    left = left_half((RANK, 2 * RHS))

    def far(a):
        picked = []
        for j in range(INTER):
            slot = recv_ref[0, a * INTER + j]
            use_left = (slot & 1) == 0
            picked.append(
                jnp.where(left == use_left, slots_ref[lax.shift_right_logical(slot, 1)], 0.0)
            )
        y = dot(coupling_ref[a], jnp.concatenate(picked, axis=0))
        return y + swap(y) + level_ref[a]

    def finish(i, carry):
        joined = jnp.where(left, far(2 * i), far(2 * i + 1))
        joined = jnp.concatenate([joined, jnp.zeros((3 * RANK, 2 * RHS), f32)], axis=0).T[:, :RANK]
        columns = block(i, 2 * LEAF)
        y = dot(joined, basis_ref[:, columns])
        y = jnp.concatenate([y[:RHS, :LEAF], y[RHS:, LEAF:]], axis=1)
        out_ref[:, columns] = near_ref[:, columns] + y
        return carry

    lax.fori_loop(0, LEAVES // 2, finish, 0)


def call(kernel, name, outs, specs, scratch, flops):
    return pl.pallas_call(
        kernel,
        name=name,
        out_shape=[jax.ShapeDtypeStruct(s, f32) for s in outs],
        in_specs=specs,
        out_specs=[vmem] * len(outs),
        scratch_shapes=scratch,
        compiler_params=pltpu.CompilerParams(vmem_limit_bytes=VMEM_BYTES),
        cost_estimate=pl.CostEstimate(flops=flops, bytes_accessed=2**20, transcendentals=0),
    )


def shards(
    charges,
    coords,
    point_order,
    near_list,
    send_list,
    recv_list,
    leaf_basis,
    local_transfer,
    leaf_coupling,
    group_transfer,
    top_coupling,
):
    place = lax.axis_index("dev").astype(jnp.int32).reshape(1)
    rows, places, first, last, coef, sent = call(
        order_kernel,
        "order",
        [
            (PTS, LEAF), (8, PTS), (PACK, LEAF), (PACK, LEAF),
            (LEAVES, RANK, 2 * RHS), (MEMBERS, 4 * RANK, 2 * RHS),
        ],
        [smem, smem, vmem, vmem, vmem],
        [pltpu.VMEM((PTS, LEAF), f32), pltpu.VMEM((8, PTS), f32)],
        10**10,
    )(point_order, send_list, charges, coords, leaf_basis)
    size = lax.axis_size("group") * lax.axis_size("dev")
    up = [(i, i + 1) for i in range(size - 1)]
    down = [(i + 1, i) for i in range(size - 1)]
    before = lax.ppermute(last, ("group", "dev"), up)
    after = lax.ppermute(first, ("group", "dev"), down)
    slots = lax.all_to_all(sent, "dev", split_axis=0, concat_axis=0, tiled=True)

    local = local_transfer.reshape(LEAVES - 1, 2, RANK, RANK)
    up_pairs = jnp.swapaxes(local, 1, 2).reshape(LEAVES - 1, RANK, 2 * RANK)
    down_pairs = jnp.swapaxes(local, 2, 3).reshape(LEAVES - 1, 2 * RANK, RANK)
    group = group_transfer.reshape(2 * MEMBERS - 2, RANK, RANK)
    group_turned = jnp.swapaxes(group, 1, 2)
    (roots,) = call(
        up_kernel,
        "up",
        [(GROUPS, RANK // 2, 2 * RHS)],
        [smem, vmem, vmem, vmem],
        [pltpu.VMEM((LEAVES * RANK, 2 * RHS), f32)],
        5 * 10**9,
    )(place, coef, up_pairs, group)
    roots = lax.all_to_all(roots, "group", split_axis=0, concat_axis=0, tiled=True)
    (tops,) = call(
        top_kernel,
        "top",
        [(MEMBERS, RANK // 2, 2 * RHS)],
        [vmem, vmem],
        [],
        10**9,
    )(roots, top_coupling)
    tops = lax.all_to_all(tops, "dev", split_axis=0, concat_axis=0, tiled=True)

    listed = jnp.pad(near_list, ((0, 0), (0, 1)))
    bias = jnp.where(jnp.arange(NEAR + 1) < NEAR, 0.0, -1e4).astype(f32)
    bias = jnp.broadcast_to(bias, listed.shape)
    (near,) = call(
        near_kernel,
        "near",
        [(RHS, PTS)],
        [smem, smem, vmem, vmem, vmem, vmem],
        [
            pltpu.VMEM((PTS, FEATURES), bf16),
            pltpu.VMEM((FEATURES, WIN), bf16),
            pltpu.VMEM((WIN, 2 * RHS), bf16),
        ],
        5 * 10**10,
    )(listed, bias, rows, places, before, after)

    coupling = jnp.swapaxes(leaf_coupling.reshape(LEAVES, INTER, RANK, RANK), 1, 2)
    coupling = coupling.reshape(LEAVES, RANK, INTER * RANK)
    (potential,) = call(
        final_kernel,
        "final",
        [(RHS, PTS)],
        [smem, smem, vmem, vmem, vmem, vmem, vmem, vmem, vmem],
        [pltpu.VMEM((LEAVES, RANK, 2 * RHS), f32)],
        10**10,
    )(
        place, recv_list, tops, group_turned, down_pairs,
        slots.reshape(4 * MEMBERS, RANK, 2 * RHS), coupling, leaf_basis, near,
    )
    return potential


def solution(mesh):
    return jax.shard_map(
        shards,
        mesh=mesh,
        in_specs=(
            P(None, ("group", "dev")),
            P(None, ("group", "dev")),
            P(("group", "dev"), None),
            P(("group", "dev"), None),
            P(("group", "dev"), None),
            P(("group", "dev"), None),
            P(None, ("group", "dev")),
            P(("group", "dev"), None),
            P(("group", "dev"), None),
            P("group", None),
            P("group", None, None),
        ),
        out_specs=P(None, ("group", "dev")),
        check_vma=False,
    )
```

```python
import functools

import jax
import jax.numpy as jnp
from jax import lax
from jax.experimental import pallas as pl
from jax.experimental.pallas import tpu as pltpu
from jax.sharding import PartitionSpec as P

f32 = jnp.float32
bf16 = jnp.bfloat16
highest = lax.Precision.HIGHEST

LEAF = 128
RANK = 32
RHS = 64
LEAVES = 32
PTS = 4096
NEAR = 27
HALO_L = 8
HALO = HALO_L * LEAF
WIN_L = LEAVES + 2 * HALO_L
WIN = WIN_L * LEAF
INTER = 8
GROUPS = 8
MEMBERS = 32
PATH = 5
FEATURES = 48

LOG2E = 1.4426950408889634
SCALE = LOG2E * 3.0**0.5 / 0.3
FLOOR = SCALE * SCALE * 1e-6
WEIGHT = 0.1 / LOG2E
DOWN = 2.0**0.5
VMEM_BYTES = 48 * 1024 * 1024

vmem = pl.BlockSpec(memory_space=pltpu.VMEM)
smem = pl.BlockSpec(memory_space=pltpu.SMEM)


def block(index, size):
    return pl.ds(pl.multiple_of(index * size, size), size)


def dot(a, b):
    return jnp.dot(a, b, precision=highest, preferred_element_type=f32)


def left_half(shape):
    return lax.broadcasted_iota(jnp.int32, shape, len(shape) - 1) < RHS


def swap(x):
    return pltpu.roll(x, RHS, 1)


def both(x):
    return jnp.where(left_half(x.shape), x, swap(x))


def fold(x):
    half = RANK // 2
    return jnp.where(left_half((half, 2 * RHS)), x[:half], swap(x[half:]))


def unfold(x):
    return jnp.concatenate([x, swap(x)], axis=0)


def two(x):
    high = x.astype(bf16)
    return high, (x - high.astype(f32)).astype(bf16)


def three(x):
    high = x.astype(bf16).astype(f32)
    rest = x - high
    middle = rest.astype(bf16).astype(f32)
    return high, middle, rest - middle


def spread(rows, ref, first):
    for c in range(RANK // 4):
        tile = rows[:, c * LEAF : (c + 1) * LEAF]
        for k in range(4):
            turned = tile if k == 0 else pltpu.roll(tile, LEAF - RANK * k, 1)
            ref[pl.ds(first * RANK + 4 * c + k, 8, stride=RANK), :] = turned


def matrix(ref, index):
    return ref[block(index, RANK), :RANK]


def spread_all(source_ref, ref, count):
    for first in range(0, count - 7, 8):
        spread(source_ref[first : first + 8, :], ref, first)
    if count % 8:
        spread(source_ref[count - 8 : count, :], ref, count - 8)


def spread_path(position, group_ref, rows_ref, ref):
    offset, count = 0, MEMBERS
    for i in range(8):
        if i < PATH:
            row = group_ref[pl.ds(offset + lax.shift_right_logical(position, i), 1), :]
            offset, count = offset + count, count // 2
        rows_ref[i : i + 1, :] = row
    spread(rows_ref[...], ref, 0)


def order_kernel(
    order_ref, charges_ref, coords_ref, basis_ref,
    points_ref, first_ref, last_ref, coef_ref,
    turned_ref, rows_ref, padded_ref,
):
    padded_ref[...] = jnp.zeros_like(padded_ref)
    padded_ref[0:3, :] = coords_ref[...]

    def turn(b, carry):
        columns = block(b, LEAF)
        tall = jnp.concatenate(
            [charges_ref[:, columns], padded_ref[:, columns], jnp.zeros((56, LEAF), f32)], axis=0
        )
        turned_ref[columns, :] = tall.T
        return carry

    lax.fori_loop(0, LEAVES, turn, 0, unroll=4)

    def fetch(b, carry):
        for i in range(64):
            at = b * 64 + i
            rows_ref[pl.ds(at, 1), :] = turned_ref[pl.ds(order_ref[0, at], 1), :]
        return carry

    lax.fori_loop(0, PTS // 64, fetch, 0)

    def coefficient(l, carry):
        columns = block(l, LEAF)
        rows = rows_ref[columns, :]
        high, low = two(rows)
        basis_high, basis_low = two(basis_ref[:, columns])
        y = jnp.dot(
            jnp.concatenate([basis_high, basis_low], axis=0),
            jnp.concatenate([high, low], axis=1),
            preferred_element_type=f32,
        )
        y = y[:RANK, : 2 * RHS] + y[:RANK, 2 * RHS :] + y[RANK:, : 2 * RHS]
        coef_ref[l] = both(y)
        points_ref[:, columns] = rows.T[: RHS + 8]
        return carry

    lax.fori_loop(0, LEAVES, coefficient, 0, unroll=4)

    first_ref[...] = points_ref[:, :HALO]
    last_ref[...] = points_ref[:, PTS - HALO :]


def up_kernel(
    place_ref, send_ref, coef_ref, local_in_ref, group_ref,
    sent_ref, level_ref, local_ref, path_in_ref, path_ref,
):
    spread_all(local_in_ref, local_ref, 2 * LEAVES - 2)
    spread_path(place_ref[0], group_ref, path_in_ref, path_ref)
    level_ref[...] = coef_ref[...]
    offset, count = 0, LEAVES
    while count > 1:
        values = [
            dot(matrix(local_ref, offset + 2 * i), level_ref[2 * i])
            + dot(matrix(local_ref, offset + 2 * i + 1), level_ref[2 * i + 1])
            for i in range(count // 2)
        ]
        for i, value in enumerate(values):
            level_ref[i] = value
        offset, count = offset + count, count // 2
    value = level_ref[0]
    for i in range(PATH):
        value = dot(matrix(path_ref, i), value)
    packed = fold(value)
    left = left_half((RANK, 2 * RHS))

    def pack(d, carry):
        for q in range(4):
            one = coef_ref[send_ref[0, d * 8 + 2 * q]]
            other = coef_ref[send_ref[0, d * 8 + 2 * q + 1]]
            sent_ref[d, q * RANK : (q + 1) * RANK, :] = jnp.where(left, one, other)
        sent_ref[d, 4 * RANK :, :] = packed
        return carry

    lax.fori_loop(0, MEMBERS, pack, 0, unroll=4)


def near_kernel(
    list_ref, points_ref, before_ref, after_ref,
    out_ref, target_ref, source_ref, weight_ref,
):
    row = lax.broadcasted_iota(jnp.int32, (8, LEAF), 0)
    zero = jnp.zeros((8, LEAF), f32)

    def prepare(w, x, own):
        columns = block(w, LEAF)
        weight_ref[:, columns] = jnp.concatenate(two(x[:RHS] * WEIGHT), axis=0)
        c = jnp.where(row < 3, (x[RHS:] - 0.5) * SCALE, 0.0)
        squares = jnp.sum(c * c, axis=0, keepdims=True) + 0.5 * FLOOR
        parts = three(jnp.broadcast_to(squares, (8, LEAF)))
        h, m, l = three(c)
        norm = jnp.where(row == 3, parts[0], jnp.where(row == 4, parts[1], parts[2]))
        is_norm = jnp.logical_and(row >= 3, row < 6)
        norm = jnp.where(is_norm, norm, 0.0)
        ones = jnp.where(is_norm, 1.0, 0.0)
        source = jnp.concatenate([h + ones, m + norm, l, h, m, h] + [zero] * 10, axis=0)
        source_ref[columns, :] = source.T[:, :FEATURES].astype(bf16)
        if own:
            target = jnp.concatenate(
                [-2.0 * h + norm, -2.0 * h + ones, -2.0 * h, -2.0 * m, -2.0 * m, -2.0 * l], axis=0
            )
            target_ref[:, block(w - HALO_L, LEAF)] = target.astype(bf16)

    def own(b, carry):
        prepare(b + HALO_L, points_ref[:, block(b, LEAF)], True)
        return carry

    lax.fori_loop(0, LEAVES, own, 0, unroll=4)
    for i in range(HALO_L):
        columns = slice(i * LEAF, (i + 1) * LEAF)
        prepare(i, before_ref[:, columns], False)
        prepare(HALO_L + LEAVES + i, after_ref[:, columns], False)

    def leaf(a, carry):
        columns = block(a, LEAF)
        target = target_ref[:, columns]
        at = [block(list_ref[a, j], LEAF) for j in range(NEAR)]
        source = jnp.concatenate([source_ref[s, :] for s in at], axis=0)
        weight = jnp.concatenate([weight_ref[:, s] for s in at], axis=1)
        squared = jnp.dot(source, target, preferred_element_type=f32)
        parts = []
        for j in range(NEAR):
            r = jnp.maximum(squared[j * LEAF : (j + 1) * LEAF], FLOOR)
            t = r * lax.rsqrt(r)
            parts.append(jnp.concatenate(two((t + LOG2E) * jnp.exp2(-t)), axis=1))
        total = jnp.dot(weight, jnp.concatenate(parts, axis=0), preferred_element_type=f32)
        out_ref[:, columns] = total[:RHS, :LEAF] + total[RHS:, :LEAF] + total[:RHS, LEAF:]
        return carry

    lax.fori_loop(0, LEAVES, leaf, 0, unroll=4)


def weights_kernel(
    place_ref, coupling_in_ref, local_in_ref, group_ref, basis_ref,
    coupling_ref, wide_basis_ref, wide_ref, local_ref, path_in_ref, path_ref,
):
    spread_all(local_in_ref, local_ref, 2 * LEAVES - 2)
    spread_path(place_ref[0], group_ref, path_in_ref, path_ref)

    def leaf(a, carry):
        spread(coupling_in_ref[block(a, INTER), :], wide_ref, a * INTER)
        return carry

    lax.fori_loop(0, LEAVES, leaf, 0, unroll=2)

    def join(a, carry):
        joined = jnp.concatenate([matrix(wide_ref, a * INTER + j) for j in range(INTER)], axis=1)
        coupling_ref[a] = jnp.concatenate(two(joined), axis=0)
        return carry

    lax.fori_loop(0, LEAVES, join, 0, unroll=2)

    node = matrix(path_ref, 0)
    for i in range(1, PATH):
        node = dot(matrix(path_ref, i), node)
    nodes = [node]
    offset = 2 * LEAVES - 4
    while len(nodes) < LEAVES:
        nodes = [
            dot(node, matrix(local_ref, offset + 2 * i + k))
            for i, node in enumerate(nodes)
            for k in (0, 1)
        ]
        offset = offset - 2 * len(nodes)
    gain = DOWN ** (2 * PATH)
    for i, node in enumerate(nodes):
        columns = slice(i * LEAF, (i + 1) * LEAF)
        carried = gain * dot(node, basis_ref[:, columns])
        wide_basis_ref[:, columns] = jnp.concatenate(two(carried), axis=0)


def root_kernel(slots_ref, out_ref, parts_ref, sem):
    copy = pltpu.make_async_copy(slots_ref.at[:, 4 * RANK :, :], parts_ref, sem)
    copy.start()
    copy.wait()
    packed = jnp.sum(parts_ref[...], axis=0)
    for g in range(GROUPS):
        out_ref[g] = packed


def turned_parts(x):
    high = x.astype(bf16).astype(f32)
    stacked = jnp.concatenate([high, x - high, high, jnp.zeros_like(high)], axis=0)
    return stacked.T.astype(bf16)


def far_kernel(recv_ref, slots_ref, coupling_ref, basis_ref, near_ref, out_ref):
    left = left_half((RANK, 2 * RHS))

    def far(a):
        picked = []
        for j in range(INTER):
            slot = recv_ref[0, a * INTER + j]
            use_left = (slot & 1) == 0
            rows = block(lax.shift_right_logical(slot, 1) & 3, RANK)
            picked.append(
                jnp.where(left == use_left, slots_ref[lax.shift_right_logical(slot, 3), rows, :], 0.0)
            )
        high, low = two(jnp.concatenate(picked, axis=0))
        y = jnp.dot(
            coupling_ref[a], jnp.concatenate([high, low], axis=1), preferred_element_type=f32
        )
        y = y[:RANK, : 2 * RHS] + y[:RANK, 2 * RHS :] + y[RANK:, : 2 * RHS]
        return y + swap(y)

    def finish(i, carry):
        turned = turned_parts(jnp.where(left, far(2 * i), far(2 * i + 1)))
        for k in (0, 1):
            columns = block(2 * i + k, LEAF)
            basis_high, basis_low = two(basis_ref[:, columns])
            basis = jnp.concatenate([basis_high, basis_high, basis_low, basis_low], axis=0)
            y = jnp.dot(turned[RHS * k : RHS * (k + 1)], basis, preferred_element_type=f32)
            out_ref[:, columns] = near_ref[:, columns] + y
        return carry

    lax.fori_loop(0, LEAVES // 2, finish, 0, unroll=4)


def final_kernel(roots_ref, top_ref, wide_basis_ref, partial_ref, out_ref):
    stacked = jnp.concatenate([unfold(roots_ref[g]) for g in range(GROUPS)], axis=0)
    turned = turned_parts(dot(top_ref[0], stacked))[:RHS]
    for start in range(0, PTS, 512):
        columns = slice(start, start + 512)
        high, low = wide_basis_ref[:RANK, columns], wide_basis_ref[RANK:, columns]
        basis = jnp.concatenate([high, high, low, low], axis=0)
        y = jnp.dot(turned, basis, preferred_element_type=f32)
        out_ref[:, columns] = partial_ref[:, columns] + y


def call(kernel, name, outs, specs, scratch, kind=f32):
    return pl.pallas_call(
        kernel,
        name=name,
        out_shape=[jax.ShapeDtypeStruct(s, kind) for s in outs],
        in_specs=specs,
        out_specs=[vmem] * len(outs),
        scratch_shapes=scratch,
        compiler_params=pltpu.CompilerParams(vmem_limit_bytes=VMEM_BYTES),
        cost_estimate=pl.CostEstimate(flops=10**9, bytes_accessed=2**20, transcendentals=0),
    )


def shards(
    charges,
    coords,
    point_order,
    near_list,
    send_list,
    recv_list,
    leaf_basis,
    local_transfer,
    leaf_coupling,
    group_transfer,
    top_coupling,
):
    place = lax.axis_index("dev").astype(jnp.int32).reshape(1)
    wide = [
        pltpu.VMEM(((2 * LEAVES - 2) * RANK, LEAF), f32),
        pltpu.VMEM((8, RANK * RANK), f32),
        pltpu.VMEM((8 * RANK, LEAF), f32),
    ]
    points, first, last, coef = call(
        order_kernel,
        "order",
        [(RHS + 8, PTS), (RHS + 8, HALO), (RHS + 8, HALO), (LEAVES, RANK, 2 * RHS)],
        [smem] + [vmem] * 3,
        [
            pltpu.VMEM((PTS, LEAF), f32),
            pltpu.VMEM((PTS, LEAF), f32),
            pltpu.VMEM((8, PTS), f32),
        ],
    )(point_order, charges, coords, leaf_basis)
    (sent,) = call(
        up_kernel,
        "up",
        [(MEMBERS, 4 * RANK + 16, 2 * RHS)],
        [smem] * 2 + [vmem] * 3,
        [pltpu.VMEM((LEAVES, RANK, 2 * RHS), f32)] + wide,
    )(place, send_list, coef, local_transfer, group_transfer)
    size = lax.axis_size("group") * lax.axis_size("dev")
    up = [(i, i + 1) for i in range(size - 1)]
    back = [(i + 1, i) for i in range(size - 1)]
    before = lax.ppermute(last, ("group", "dev"), up)
    after = lax.ppermute(first, ("group", "dev"), back)
    sent, before, after = lax.optimization_barrier((sent, before, after))
    slots = lax.all_to_all(sent, "dev", split_axis=0, concat_axis=0, tiled=True)
    (near,) = call(
        near_kernel,
        "near",
        [(RHS, PTS)],
        [smem, vmem, vmem, vmem],
        [
            pltpu.VMEM((FEATURES, PTS), bf16),
            pltpu.VMEM((WIN, FEATURES), bf16),
            pltpu.VMEM((2 * RHS, WIN), bf16),
        ],
    )(near_list, points, before, after)

    coupling, wide_basis = call(
        weights_kernel,
        "weights",
        [(LEAVES, 2 * RANK, INTER * RANK), (2 * RANK, PTS)],
        [smem] + [vmem] * 4,
        [pltpu.VMEM((LEAVES * INTER * RANK, LEAF), f32)] + wide,
        bf16,
    )(place, leaf_coupling, local_transfer, group_transfer, leaf_basis)
    (roots,) = call(
        root_kernel,
        "root",
        [(GROUPS, RANK // 2, 2 * RHS)],
        [pl.BlockSpec(memory_space=pl.ANY)],
        [pltpu.VMEM((MEMBERS, RANK // 2, 2 * RHS), f32), pltpu.SemaphoreType.DMA],
    )(slots)
    roots, slots = lax.optimization_barrier((roots, slots))
    roots = lax.all_to_all(roots, "group", split_axis=0, concat_axis=0, tiled=True)
    (partial,) = call(
        far_kernel, "far", [(RHS, PTS)], [smem] + [vmem] * 4, []
    )(recv_list, slots, coupling, leaf_basis, near)
    (potential,) = call(
        final_kernel, "final", [(RHS, PTS)], [vmem] * 4, []
    )(roots, top_coupling, wide_basis, partial)
    return potential


def solution(mesh):
    return jax.shard_map(
        shards,
        mesh=mesh,
        in_specs=(
            P(None, ("group", "dev")),
            P(None, ("group", "dev")),
            P(("group", "dev"), None),
            P(("group", "dev"), None),
            P(("group", "dev"), None),
            P(("group", "dev"), None),
            P(None, ("group", "dev")),
            P(("group", "dev"), None),
            P(("group", "dev"), None),
            P("group", None),
            P("group", None, None),
        ),
        out_specs=P(None, ("group", "dev")),
        check_vma=False,
    )
```

```python
import functools

import jax
import jax.numpy as jnp
from jax import lax
from jax.experimental import pallas as pl
from jax.experimental.pallas import tpu as pltpu
from jax.sharding import PartitionSpec as P

f32 = jnp.float32
bf16 = jnp.bfloat16
highest = lax.Precision.HIGHEST

LEAF = 128
RANK = 32
RHS = 64
LEAVES = 32
PTS = 4096
NEAR = 27
HALO_L = 8
HALO = HALO_L * LEAF
WIN_L = LEAVES + 2 * HALO_L
WIN = WIN_L * LEAF
INTER = 8
GROUPS = 8
MEMBERS = 32
PATH = 5
FEATURES = 48

LOG2E = 1.4426950408889634
SCALE = LOG2E * 3.0**0.5 / 0.3
FLOOR = SCALE * SCALE * 1e-6
WEIGHT = 0.1 / LOG2E
DOWN = 2.0**0.5
PART_L = HALO_L
PARTS = [slice(HALO * i, HALO * (i + 1)) for i in range(PTS // HALO)]
VMEM_BYTES = 60 * 1024 * 1024

vmem = pl.BlockSpec(memory_space=pltpu.VMEM)
hbm = pl.BlockSpec(memory_space=pl.ANY)
smem = pl.BlockSpec(memory_space=pltpu.SMEM)


def block(index, size):
    return pl.ds(pl.multiple_of(index * size, size), size)


def dot(a, b):
    return jnp.dot(a, b, precision=highest, preferred_element_type=f32)


def left_half(shape):
    return lax.broadcasted_iota(jnp.int32, shape, len(shape) - 1) < RHS


def swap(x):
    return pltpu.roll(x, RHS, 1)


def both(x):
    return jnp.where(left_half(x.shape), x, swap(x))


def fold(x):
    half = RANK // 2
    return jnp.where(left_half((half, 2 * RHS)), x[:half], swap(x[half:]))


def unfold(x):
    return jnp.concatenate([x, swap(x)], axis=0)


def two(x):
    high = x.astype(bf16)
    return high, (x - high.astype(f32)).astype(bf16)


def three(x):
    high = x.astype(bf16).astype(f32)
    rest = x - high
    middle = rest.astype(bf16).astype(f32)
    return high, middle, rest - middle


def spread(rows, ref, first):
    for c in range(RANK // 4):
        tile = rows[:, c * LEAF : (c + 1) * LEAF]
        for k in range(4):
            turned = tile if k == 0 else pltpu.roll(tile, LEAF - RANK * k, 1)
            ref[pl.ds(first * RANK + 4 * c + k, 8, stride=RANK), :] = turned


def matrix(ref, index):
    return ref[block(index, RANK), :RANK]


def spread_all(source_ref, ref, count):
    for first in range(0, count - 7, 8):
        spread(source_ref[first : first + 8, :], ref, first)
    if count % 8:
        spread(source_ref[count - 8 : count, :], ref, count - 8)


def spread_path(position, group_ref, rows_ref, ref):
    offset, count = 0, MEMBERS
    for i in range(8):
        if i < PATH:
            row = group_ref[pl.ds(offset + lax.shift_right_logical(position, i), 1), :]
            offset, count = offset + count, count // 2
        rows_ref[i : i + 1, :] = row
    spread(rows_ref[...], ref, 0)


def order_kernel(
    place_ref, order_ref, charges_hbm, coords_ref, basis_hbm, local_hbm, group_hbm,
    points_hbm, first_hbm, last_hbm, coef_hbm, roots_hbm,
    charges_ref, basis_ref, points_ref, coef_ref, turned_ref, rows_ref, padded_ref,
    level_ref, roots_ref, local_in_ref, group_ref, local_ref, path_in_ref, path_ref,
    sems, out_sems,
):
    loads = [
        pltpu.make_async_copy(charges_hbm.at[:, part], charges_ref.at[:, part], sems.at[i])
        for i, part in enumerate(PARTS)
    ]
    for source, target in ((basis_hbm, basis_ref), (local_hbm, local_in_ref), (group_hbm, group_ref)):
        loads.append(pltpu.make_async_copy(source, target, sems.at[len(loads)]))
    for load in loads:
        load.start()
    padded_ref[...] = jnp.zeros_like(padded_ref)
    padded_ref[0:3, :] = coords_ref[...]

    def turn(b, carry):
        columns = block(b, LEAF)
        tall = jnp.concatenate(
            [charges_ref[:, columns], padded_ref[:, columns], jnp.zeros((56, LEAF), f32)], axis=0
        )
        turned_ref[columns, :] = tall.T
        return carry

    for i in range(len(PARTS)):
        loads[i].wait()
        lax.fori_loop(PART_L * i, PART_L * (i + 1), turn, 0, unroll=4)

    def fetch(b, carry):
        for i in range(64):
            at = b * 64 + i
            rows_ref[pl.ds(at, 1), :] = turned_ref[pl.ds(order_ref[0, at], 1), :]
        return carry

    lax.fori_loop(0, PTS // 64, fetch, 0)

    def coefficient(l, carry):
        columns = block(l, LEAF)
        rows = rows_ref[columns, :]
        high, low = two(rows)
        basis_high, basis_low = two(basis_ref[:, columns])
        y = jnp.dot(
            jnp.concatenate([basis_high, basis_low], axis=0),
            jnp.concatenate([high, low], axis=1),
            preferred_element_type=f32,
        )
        y = y[:RANK, : 2 * RHS] + y[:RANK, 2 * RHS :] + y[RANK:, : 2 * RHS]
        coef_ref[l] = both(y)
        points_ref[:, columns] = rows.T[: RHS + 8]
        return carry

    for load in loads[len(PARTS) :]:
        load.wait()
    stores = []

    def store(source, target):
        copy = pltpu.make_async_copy(source, target, out_sems.at[len(stores)])
        copy.start()
        stores.append(copy)

    for i, part in enumerate(PARTS):
        lax.fori_loop(PART_L * i, PART_L * (i + 1), coefficient, 0, unroll=4)
        leaves = slice(PART_L * i, PART_L * (i + 1))
        store(coef_ref.at[leaves], coef_hbm.at[leaves])
        store(points_ref.at[:, part], points_hbm.at[:, part])
        if i == 0:
            store(points_ref.at[:, part], first_hbm)
        if i == len(PARTS) - 1:
            store(points_ref.at[:, part], last_hbm)

    spread_all(local_in_ref, local_ref, 2 * LEAVES - 2)
    spread_path(place_ref[0], group_ref, path_in_ref, path_ref)
    nodes = coef_ref
    offset, count = 0, LEAVES
    while count > 1:
        values = [
            dot(matrix(local_ref, offset + 2 * i), nodes[2 * i])
            + dot(matrix(local_ref, offset + 2 * i + 1), nodes[2 * i + 1])
            for i in range(count // 2)
        ]
        nodes = level_ref
        for i, value in enumerate(values):
            level_ref[i] = value
        offset, count = offset + count, count // 2
    value = level_ref[0]
    for i in range(PATH):
        value = dot(matrix(path_ref, i), value)
    packed = fold(value)
    for g in range(GROUPS):
        roots_ref[g] = packed
    store(roots_ref, roots_hbm)
    for copy in stores:
        copy.wait()


def top_kernel(roots_ref, top_ref, sent_in_hbm, sent_hbm, tops_ref, sem):
    stacked = jnp.concatenate([unfold(roots_ref[g]) for g in range(GROUPS)], axis=0)
    packed = fold(dot(top_ref[0], stacked))
    for d in range(MEMBERS):
        tops_ref[d] = packed
    copy = pltpu.make_async_copy(tops_ref, sent_hbm.at[:, 4 * RANK :, :], sem)
    copy.start()
    copy.wait()


def pack_kernel(send_ref, coef_hbm, sent_hbm, coef_ref, sent_ref, sems):
    load = pltpu.make_async_copy(coef_hbm, coef_ref, sems.at[0])
    load.start()
    left = left_half((RANK, 2 * RHS))
    load.wait()

    def pack(d, carry):
        for q in range(4):
            one = coef_ref[send_ref[0, d * 8 + 2 * q]]
            other = coef_ref[send_ref[0, d * 8 + 2 * q + 1]]
            sent_ref[d, q * RANK : (q + 1) * RANK, :] = jnp.where(left, one, other)
        return carry

    stores = []
    for i in range(4):
        lax.fori_loop(8 * i, 8 * (i + 1), pack, 0, unroll=4)
        some = slice(8 * i, 8 * (i + 1))
        copy = pltpu.make_async_copy(
            sent_ref.at[some], sent_hbm.at[some, : 4 * RANK, :], sems.at[i + 1]
        )
        copy.start()
        stores.append(copy)
    for copy in stores:
        copy.wait()


def near_kernel(
    list_ref, points_ref, before_ref, after_ref,
    out_ref, target_ref, source_ref, weight_ref,
):
    row = lax.broadcasted_iota(jnp.int32, (8, LEAF), 0)
    zero = jnp.zeros((8, LEAF), f32)

    def prepare(w, x, own):
        columns = block(w, LEAF)
        weight_ref[:, columns] = jnp.concatenate(two(x[:RHS] * WEIGHT), axis=0)
        c = jnp.where(row < 3, (x[RHS:] - 0.5) * SCALE, 0.0)
        squares = jnp.sum(c * c, axis=0, keepdims=True) + 0.5 * FLOOR
        parts = three(jnp.broadcast_to(squares, (8, LEAF)))
        h, m, l = three(c)
        norm = jnp.where(row == 3, parts[0], jnp.where(row == 4, parts[1], parts[2]))
        is_norm = jnp.logical_and(row >= 3, row < 6)
        norm = jnp.where(is_norm, norm, 0.0)
        ones = jnp.where(is_norm, 1.0, 0.0)
        source = jnp.concatenate([h + ones, m + norm, l, h, m, h] + [zero] * 10, axis=0)
        source_ref[columns, :] = source.T[:, :FEATURES].astype(bf16)
        if own:
            target = jnp.concatenate(
                [-2.0 * h + norm, -2.0 * h + ones, -2.0 * h, -2.0 * m, -2.0 * m, -2.0 * l], axis=0
            )
            target_ref[:, block(w - HALO_L, LEAF)] = target.astype(bf16)

    def own(b, carry):
        prepare(b + HALO_L, points_ref[:, block(b, LEAF)], True)
        return carry

    lax.fori_loop(0, LEAVES, own, 0, unroll=4)
    for i in range(HALO_L):
        columns = slice(i * LEAF, (i + 1) * LEAF)
        prepare(i, before_ref[:, columns], False)
        prepare(HALO_L + LEAVES + i, after_ref[:, columns], False)

    def leaf(a, carry):
        columns = block(a, LEAF)
        target = target_ref[:, columns]
        at = [block(list_ref[a, j], LEAF) for j in range(NEAR)]
        source = jnp.concatenate([source_ref[s, :] for s in at], axis=0)
        weight = jnp.concatenate([weight_ref[:, s] for s in at], axis=1)
        squared = jnp.dot(source, target, preferred_element_type=f32)
        parts = []
        for j in range(NEAR):
            r = jnp.maximum(squared[j * LEAF : (j + 1) * LEAF], FLOOR)
            t = r * lax.rsqrt(r)
            parts.append(jnp.concatenate(two((t + LOG2E) * jnp.exp2(-t)), axis=1))
        total = jnp.dot(weight, jnp.concatenate(parts, axis=0), preferred_element_type=f32)
        out_ref[:, columns] = total[:RHS, :LEAF] + total[RHS:, :LEAF] + total[:RHS, LEAF:]
        return carry

    lax.fori_loop(0, LEAVES, leaf, 0, unroll=4)


def weights_kernel(
    place_ref, coupling_in_ref, local_in_ref, group_ref, basis_ref,
    coupling_ref, wide_basis_ref, wide_ref, local_ref, path_in_ref, path_ref,
):
    spread_all(local_in_ref, local_ref, 2 * LEAVES - 2)
    spread_path(place_ref[0], group_ref, path_in_ref, path_ref)

    def leaf(a, carry):
        spread(coupling_in_ref[block(a, INTER), :], wide_ref, a * INTER)
        return carry

    lax.fori_loop(0, LEAVES, leaf, 0, unroll=2)

    def join(a, carry):
        joined = jnp.concatenate([matrix(wide_ref, a * INTER + j) for j in range(INTER)], axis=1)
        coupling_ref[a] = jnp.concatenate(two(joined), axis=0)
        return carry

    lax.fori_loop(0, LEAVES, join, 0, unroll=2)

    node = matrix(path_ref, 0)
    for i in range(1, PATH):
        node = dot(matrix(path_ref, i), node)
    nodes = [node]
    offset = 2 * LEAVES - 4
    while len(nodes) < LEAVES:
        nodes = [
            dot(node, matrix(local_ref, offset + 2 * i + k))
            for i, node in enumerate(nodes)
            for k in (0, 1)
        ]
        offset = offset - 2 * len(nodes)
    gain = DOWN ** (2 * PATH)
    for i, node in enumerate(nodes):
        columns = slice(i * LEAF, (i + 1) * LEAF)
        carried = gain * dot(node, basis_ref[:, columns])
        wide_basis_ref[:, columns] = jnp.concatenate(two(carried), axis=0)


def turned_parts(x):
    high = x.astype(bf16).astype(f32)
    stacked = jnp.concatenate([high, x - high, high, jnp.zeros_like(high)], axis=0)
    return stacked.T.astype(bf16)


def far_kernel(
    recv_ref, slots_hbm, coupling_hbm, basis_hbm, wide_basis_hbm, near_hbm,
    out_hbm, slots_ref, coupling_ref, basis_ref, wide_basis_ref, near_ref, turned_ref,
    sems, out_sems,
):
    loads = [
        pltpu.make_async_copy(source, target, sems.at[i])
        for i, (source, target) in enumerate(
            (
                (slots_hbm, slots_ref),
                (coupling_hbm, coupling_ref),
                (basis_hbm, basis_ref),
                (wide_basis_hbm, wide_basis_ref),
                (near_hbm, near_ref),
            )
        )
    ]
    for load in loads:
        load.start()
    for load in loads[:2]:
        load.wait()
    top = slots_ref[0, 4 * RANK :, :]
    for d in range(1, MEMBERS):
        top = top + slots_ref[d, 4 * RANK :, :]
    top = turned_parts(unfold(top))[:RHS]
    left = left_half((RANK, 2 * RHS))

    def far(a):
        picked = []
        for j in range(INTER):
            slot = recv_ref[0, a * INTER + j]
            use_left = (slot & 1) == 0
            rows = block(lax.shift_right_logical(slot, 1) & 3, RANK)
            picked.append(
                jnp.where(left == use_left, slots_ref[lax.shift_right_logical(slot, 3), rows, :], 0.0)
            )
        high, low = two(jnp.concatenate(picked, axis=0))
        y = jnp.dot(
            coupling_ref[a], jnp.concatenate([high, low], axis=1), preferred_element_type=f32
        )
        y = y[:RANK, : 2 * RHS] + y[:RANK, 2 * RHS :] + y[RANK:, : 2 * RHS]
        return y + swap(y)

    def turn(i, carry):
        turned_ref[i] = turned_parts(jnp.where(left, far(2 * i), far(2 * i + 1)))
        return carry

    lax.fori_loop(0, LEAVES // 2, turn, 0, unroll=8)
    for load in loads[2:]:
        load.wait()

    def finish(a, carry):
        columns = block(a, LEAF)
        basis_high, basis_low = two(basis_ref[:, columns])
        high, low = wide_basis_ref[:RANK, columns], wide_basis_ref[RANK:, columns]
        basis = jnp.concatenate(
            [basis_high, basis_high, basis_low, basis_low, high, high, low, low], axis=0
        )
        rows = turned_ref[lax.shift_right_logical(a, 1), block(a & 1, RHS), :]
        joined = jnp.concatenate([rows, top], axis=1)
        y = jnp.dot(joined, basis, preferred_element_type=f32)
        near_ref[:, columns] = near_ref[:, columns] + y
        return carry

    stores = []
    for i, part in enumerate(PARTS):
        lax.fori_loop(PART_L * i, PART_L * (i + 1), finish, 0, unroll=8)
        copy = pltpu.make_async_copy(near_ref.at[:, part], out_hbm.at[:, part], out_sems.at[i])
        copy.start()
        stores.append(copy)
    for copy in stores:
        copy.wait()


def call(kernel, name, outs, specs, scratch, kind=f32, out=vmem, aliases=None):
    return pl.pallas_call(
        kernel,
        name=name,
        out_shape=[jax.ShapeDtypeStruct(s, kind) for s in outs],
        in_specs=specs,
        out_specs=[out] * len(outs),
        scratch_shapes=scratch,
        input_output_aliases=aliases or {},
        compiler_params=pltpu.CompilerParams(vmem_limit_bytes=VMEM_BYTES),
        cost_estimate=pl.CostEstimate(flops=10**9, bytes_accessed=2**20, transcendentals=0),
    )


def shards(
    charges,
    coords,
    point_order,
    near_list,
    send_list,
    recv_list,
    leaf_basis,
    local_transfer,
    leaf_coupling,
    group_transfer,
    top_coupling,
):
    place = lax.axis_index("dev").astype(jnp.int32).reshape(1)
    wide = [
        pltpu.VMEM(((2 * LEAVES - 2) * RANK, LEAF), f32),
        pltpu.VMEM((8, RANK * RANK), f32),
        pltpu.VMEM((8 * RANK, LEAF), f32),
    ]
    points, first, last, coef, roots = call(
        order_kernel,
        "order",
        [
            (RHS + 8, PTS), (RHS + 8, HALO), (RHS + 8, HALO),
            (LEAVES, RANK, 2 * RHS), (GROUPS, RANK // 2, 2 * RHS),
        ],
        [smem, smem, hbm, vmem, hbm, hbm, hbm],
        [
            pltpu.VMEM((RHS, PTS), f32),
            pltpu.VMEM((RANK, PTS), f32),
            pltpu.VMEM((RHS + 8, PTS), f32),
            pltpu.VMEM((LEAVES, RANK, 2 * RHS), f32),
            pltpu.VMEM((PTS, LEAF), f32),
            pltpu.VMEM((PTS, LEAF), f32),
            pltpu.VMEM((8, PTS), f32),
            pltpu.VMEM((LEAVES // 2, RANK, 2 * RHS), f32),
            pltpu.VMEM((GROUPS, RANK // 2, 2 * RHS), f32),
            pltpu.VMEM((2 * LEAVES - 2, RANK * RANK), f32),
            pltpu.VMEM((2 * MEMBERS - 2, RANK * RANK), f32),
        ]
        + wide
        + [
            pltpu.SemaphoreType.DMA((len(PARTS) + 3,)),
            pltpu.SemaphoreType.DMA((2 * len(PARTS) + 3,)),
        ],
        out=hbm,
    )(place, point_order, charges, coords, leaf_basis, local_transfer, group_transfer)
    (sent,) = call(
        pack_kernel,
        "pack",
        [(MEMBERS, 4 * RANK + RANK // 2, 2 * RHS)],
        [smem, hbm],
        [
            pltpu.VMEM((LEAVES, RANK, 2 * RHS), f32),
            pltpu.VMEM((MEMBERS, 4 * RANK, 2 * RHS), f32),
            pltpu.SemaphoreType.DMA((5,)),
        ],
        out=hbm,
    )(send_list, coef)
    roots = lax.all_to_all(roots, "group", split_axis=0, concat_axis=0, tiled=True)
    size = lax.axis_size("group") * lax.axis_size("dev")
    up = [(i, i + 1) for i in range(size - 1)]
    back = [(i + 1, i) for i in range(size - 1)]
    before = lax.ppermute(last, ("group", "dev"), up)
    after = lax.ppermute(first, ("group", "dev"), back)
    roots, before, after = lax.optimization_barrier((roots, before, after))
    (sent,) = call(
        top_kernel,
        "top",
        [sent.shape],
        [vmem, vmem, hbm],
        [pltpu.VMEM((MEMBERS, RANK // 2, 2 * RHS), f32), pltpu.SemaphoreType.DMA],
        out=hbm,
        aliases={2: 0},
    )(roots, top_coupling, sent)
    slots = lax.all_to_all(sent, "dev", split_axis=0, concat_axis=0, tiled=True)
    (near,) = call(
        near_kernel,
        "near",
        [(RHS, PTS)],
        [smem, vmem, vmem, vmem],
        [
            pltpu.VMEM((FEATURES, PTS), bf16),
            pltpu.VMEM((WIN, FEATURES), bf16),
            pltpu.VMEM((2 * RHS, WIN), bf16),
        ],
    )(near_list, points, before, after)

    coupling, wide_basis = call(
        weights_kernel,
        "weights",
        [(LEAVES, 2 * RANK, INTER * RANK), (2 * RANK, PTS)],
        [smem] + [vmem] * 4,
        [pltpu.VMEM((LEAVES * INTER * RANK, LEAF), f32)] + wide,
        bf16,
    )(place, leaf_coupling, local_transfer, group_transfer, leaf_basis)
    (potential,) = call(
        far_kernel,
        "far",
        [(RHS, PTS)],
        [smem] + [hbm] * 5,
        [
            pltpu.VMEM((MEMBERS, 4 * RANK + RANK // 2, 2 * RHS), f32),
            pltpu.VMEM((LEAVES, 2 * RANK, INTER * RANK), bf16),
            pltpu.VMEM((RANK, PTS), f32),
            pltpu.VMEM((2 * RANK, PTS), bf16),
            pltpu.VMEM((RHS, PTS), f32),
            pltpu.VMEM((LEAVES // 2, 2 * RHS, 2 * RHS), bf16),
            pltpu.SemaphoreType.DMA((5,)),
            pltpu.SemaphoreType.DMA((len(PARTS),)),
        ],
        out=hbm,
    )(recv_list, slots, coupling, leaf_basis, wide_basis, near)
    return potential


def solution(mesh):
    return jax.shard_map(
        shards,
        mesh=mesh,
        in_specs=(
            P(None, ("group", "dev")),
            P(None, ("group", "dev")),
            P(("group", "dev"), None),
            P(("group", "dev"), None),
            P(("group", "dev"), None),
            P(("group", "dev"), None),
            P(None, ("group", "dev")),
            P(("group", "dev"), None),
            P(("group", "dev"), None),
            P("group", None),
            P("group", None, None),
        ),
        out_specs=P(None, ("group", "dev")),
        check_vma=False,
    )
```

```python
import functools

import jax
import jax.numpy as jnp
from jax import lax
from jax.experimental import pallas as pl
from jax.experimental.pallas import tpu as pltpu
from jax.sharding import PartitionSpec as P

f32 = jnp.float32
bf16 = jnp.bfloat16
highest = lax.Precision.HIGHEST

LEAF = 128
RANK = 32
RHS = 64
LEAVES = 32
PTS = 4096
NEAR = 27
HALO_L = 8
HALO = HALO_L * LEAF
WIN_L = LEAVES + 2 * HALO_L
WIN = WIN_L * LEAF
INTER = 8
GROUPS = 8
MEMBERS = 32
PATH = 5
FEATURES = 48

LOG2E = 1.4426950408889634
SCALE = LOG2E * 3.0**0.5 / 0.3
FLOOR = SCALE * SCALE * 1e-6
WEIGHT = 0.1 / LOG2E
DOWN = 2.0**0.5
PART_L = HALO_L
PARTS = [slice(HALO * i, HALO * (i + 1)) for i in range(PTS // HALO)]
VMEM_BYTES = 60 * 1024 * 1024
LESS_VMEM = 50 * 1024 * 1024

vmem = pl.BlockSpec(memory_space=pltpu.VMEM)
hbm = pl.BlockSpec(memory_space=pl.ANY)
smem = pl.BlockSpec(memory_space=pltpu.SMEM)


def block(index, size):
    return pl.ds(pl.multiple_of(index * size, size), size)


def dot(a, b):
    return jnp.dot(a, b, precision=highest, preferred_element_type=f32)


def left_half(shape):
    return lax.broadcasted_iota(jnp.int32, shape, len(shape) - 1) < RHS


def swap(x):
    return pltpu.roll(x, RHS, 1)


def both(x):
    return jnp.where(left_half(x.shape), x, swap(x))


def fold(x):
    half = RANK // 2
    return jnp.where(left_half((half, 2 * RHS)), x[:half], swap(x[half:]))


def unfold(x):
    return jnp.concatenate([x, swap(x)], axis=0)


def two(x):
    high = x.astype(bf16)
    return high, (x - high.astype(f32)).astype(bf16)


def three(x):
    high = x.astype(bf16).astype(f32)
    rest = x - high
    middle = rest.astype(bf16).astype(f32)
    return high, middle, rest - middle


def spread(rows, ref, first):
    for c in range(RANK // 4):
        tile = rows[:, c * LEAF : (c + 1) * LEAF]
        for k in range(4):
            turned = tile if k == 0 else pltpu.roll(tile, LEAF - RANK * k, 1)
            ref[pl.ds(first * RANK + 4 * c + k, 8, stride=RANK), :] = turned


def matrix(ref, index):
    return ref[block(index, RANK), :RANK]


def spread_all(source_ref, ref, count):
    for first in range(0, count - 7, 8):
        spread(source_ref[first : first + 8, :], ref, first)
    if count % 8:
        spread(source_ref[count - 8 : count, :], ref, count - 8)


def spread_path(position, group_ref, rows_ref, ref):
    offset, count = 0, MEMBERS
    for i in range(8):
        if i < PATH:
            row = group_ref[pl.ds(offset + lax.shift_right_logical(position, i), 1), :]
            offset, count = offset + count, count // 2
        rows_ref[i : i + 1, :] = row
    spread(rows_ref[...], ref, 0)


def order_kernel(
    place_ref, order_ref, charges_hbm, coords_ref, basis_hbm, local_hbm, group_hbm,
    points_hbm, first_hbm, last_hbm, coef_hbm, roots_hbm,
    charges_ref, basis_ref, points_ref, coef_ref, turned_ref, rows_ref, padded_ref,
    level_ref, roots_ref, local_in_ref, group_ref, local_ref, path_in_ref, path_ref,
    sems, out_sems,
):
    loads = [
        pltpu.make_async_copy(charges_hbm.at[:, part], charges_ref.at[:, part], sems.at[i])
        for i, part in enumerate(PARTS)
    ]
    for source, target in ((basis_hbm, basis_ref), (local_hbm, local_in_ref), (group_hbm, group_ref)):
        loads.append(pltpu.make_async_copy(source, target, sems.at[len(loads)]))
    for load in loads:
        load.start()
    padded_ref[...] = jnp.zeros_like(padded_ref)
    padded_ref[0:3, :] = coords_ref[...]

    def turn(b, carry):
        columns = block(b, LEAF)
        tall = jnp.concatenate(
            [charges_ref[:, columns], padded_ref[:, columns], jnp.zeros((56, LEAF), f32)], axis=0
        )
        turned_ref[columns, :] = tall.T
        return carry

    for i in range(len(PARTS)):
        loads[i].wait()
        lax.fori_loop(PART_L * i, PART_L * (i + 1), turn, 0, unroll=4)

    def fetch(b, carry):
        for i in range(64):
            at = b * 64 + i
            rows_ref[pl.ds(at, 1), :] = turned_ref[pl.ds(order_ref[0, at], 1), :]
        return carry

    lax.fori_loop(0, PTS // 64, fetch, 0)

    def coefficient(l, carry):
        columns = block(l, LEAF)
        rows = rows_ref[columns, :]
        high, low = two(rows)
        basis_high, basis_low = two(basis_ref[:, columns])
        y = jnp.dot(
            jnp.concatenate([basis_high, basis_low], axis=0),
            jnp.concatenate([high, low], axis=1),
            preferred_element_type=f32,
        )
        y = y[:RANK, : 2 * RHS] + y[:RANK, 2 * RHS :] + y[RANK:, : 2 * RHS]
        coef_ref[l] = both(y)
        points_ref[:, columns] = rows.T[: RHS + 8]
        return carry

    for load in loads[len(PARTS) :]:
        load.wait()
    stores = []

    def store(source, target):
        copy = pltpu.make_async_copy(source, target, out_sems.at[len(stores)])
        copy.start()
        stores.append(copy)

    for i, part in enumerate(PARTS):
        lax.fori_loop(PART_L * i, PART_L * (i + 1), coefficient, 0, unroll=4)
        leaves = slice(PART_L * i, PART_L * (i + 1))
        store(coef_ref.at[leaves], coef_hbm.at[leaves])
        store(points_ref.at[:, part], points_hbm.at[:, part])
        if i == 0:
            store(points_ref.at[:, part], first_hbm)
        if i == len(PARTS) - 1:
            store(points_ref.at[:, part], last_hbm)

    spread_all(local_in_ref, local_ref, 2 * LEAVES - 2)
    spread_path(place_ref[0], group_ref, path_in_ref, path_ref)
    low, middle, high = (matrix(path_ref, i) for i in (0, 2, 4))
    path = dot(
        dot(high, matrix(path_ref, 3)), dot(middle, dot(matrix(path_ref, 1), low))
    )
    nodes = coef_ref
    offset, count = 0, LEAVES
    while count > 1:
        values = [
            dot(matrix(local_ref, offset + 2 * i), nodes[2 * i])
            + dot(matrix(local_ref, offset + 2 * i + 1), nodes[2 * i + 1])
            for i in range(count // 2)
        ]
        nodes = level_ref
        for i, value in enumerate(values):
            level_ref[i] = value
        offset, count = offset + count, count // 2
    packed = fold(dot(path, level_ref[0]))
    for g in range(GROUPS):
        roots_ref[g] = packed
    store(roots_ref, roots_hbm)
    for copy in stores:
        copy.wait()


def top_kernel(roots_ref, top_ref, sent_in_hbm, sent_hbm, tops_ref, sem):
    stacked = jnp.concatenate([unfold(roots_ref[g]) for g in range(GROUPS)], axis=0)
    packed = fold(dot(top_ref[0], stacked))
    for d in range(MEMBERS):
        tops_ref[d] = packed
    copy = pltpu.make_async_copy(tops_ref, sent_hbm.at[:, 4 * RANK :, :], sem)
    copy.start()
    copy.wait()


def pack_kernel(send_ref, coef_hbm, sent_hbm, coef_ref, sent_ref, sems):
    load = pltpu.make_async_copy(coef_hbm, coef_ref, sems.at[0])
    load.start()
    left = left_half((RANK, 2 * RHS))
    load.wait()

    def pack(d, carry):
        for q in range(4):
            one = coef_ref[send_ref[0, d * 8 + 2 * q]]
            other = coef_ref[send_ref[0, d * 8 + 2 * q + 1]]
            sent_ref[d, q * RANK : (q + 1) * RANK, :] = jnp.where(left, one, other)
        return carry

    stores = []
    for i in range(4):
        lax.fori_loop(8 * i, 8 * (i + 1), pack, 0, unroll=4)
        some = slice(8 * i, 8 * (i + 1))
        copy = pltpu.make_async_copy(
            sent_ref.at[some], sent_hbm.at[some, : 4 * RANK, :], sems.at[i + 1]
        )
        copy.start()
        stores.append(copy)
    for copy in stores:
        copy.wait()


def near_kernel(
    list_ref, points_ref, before_ref, after_ref,
    out_ref, target_ref, source_ref, weight_ref,
):
    row = lax.broadcasted_iota(jnp.int32, (8, LEAF), 0)
    zero = jnp.zeros((8, LEAF), f32)

    def prepare(w, x, own):
        columns = block(w, LEAF)
        weight_ref[:, columns] = jnp.concatenate(two(x[:RHS] * WEIGHT), axis=0)
        c = jnp.where(row < 3, (x[RHS:] - 0.5) * SCALE, 0.0)
        squares = jnp.sum(c * c, axis=0, keepdims=True) + 0.5 * FLOOR
        parts = three(jnp.broadcast_to(squares, (8, LEAF)))
        h, m, l = three(c)
        norm = jnp.where(row == 3, parts[0], jnp.where(row == 4, parts[1], parts[2]))
        is_norm = jnp.logical_and(row >= 3, row < 6)
        norm = jnp.where(is_norm, norm, 0.0)
        ones = jnp.where(is_norm, 1.0, 0.0)
        source = jnp.concatenate([h + ones, m + norm, l, h, m, h] + [zero] * 10, axis=0)
        source_ref[columns, :] = source.T[:, :FEATURES].astype(bf16)
        if own:
            target = jnp.concatenate(
                [-2.0 * h + norm, -2.0 * h + ones, -2.0 * h, -2.0 * m, -2.0 * m, -2.0 * l], axis=0
            )
            target_ref[:, block(w - HALO_L, LEAF)] = target.astype(bf16)

    def own(b, carry):
        prepare(b + HALO_L, points_ref[:, block(b, LEAF)], True)
        return carry

    lax.fori_loop(0, LEAVES, own, 0, unroll=4)
    for i in range(HALO_L):
        columns = slice(i * LEAF, (i + 1) * LEAF)
        prepare(i, before_ref[:, columns], False)
        prepare(HALO_L + LEAVES + i, after_ref[:, columns], False)

    def leaf(a, carry):
        columns = block(a, LEAF)
        target = target_ref[:, columns]
        at = [block(list_ref[a, j], LEAF) for j in range(NEAR)]
        source = jnp.concatenate([source_ref[s, :] for s in at], axis=0)
        weight = jnp.concatenate([weight_ref[:, s] for s in at], axis=1)
        squared = jnp.dot(source, target, preferred_element_type=f32)
        parts = []
        for j in range(NEAR):
            r = jnp.maximum(squared[j * LEAF : (j + 1) * LEAF], FLOOR)
            t = r * lax.rsqrt(r)
            parts.append(jnp.concatenate(two((t + LOG2E) * jnp.exp2(-t)), axis=1))
        total = jnp.dot(weight, jnp.concatenate(parts, axis=0), preferred_element_type=f32)
        out_ref[:, columns] = total[:RHS, :LEAF] + total[RHS:, :LEAF] + total[:RHS, LEAF:]
        return carry

    lax.fori_loop(0, LEAVES, leaf, 0, unroll=4)


def weights_kernel(
    place_ref, coupling_in_ref, local_in_ref, group_ref, basis_ref,
    coupling_ref, wide_basis_ref, wide_ref, local_ref, path_in_ref, path_ref,
):
    spread_all(local_in_ref, local_ref, 2 * LEAVES - 2)
    spread_path(place_ref[0], group_ref, path_in_ref, path_ref)

    def leaf(a, carry):
        spread(coupling_in_ref[block(a, INTER), :], wide_ref, a * INTER)
        return carry

    lax.fori_loop(0, LEAVES, leaf, 0, unroll=2)

    def join(a, carry):
        joined = jnp.concatenate([matrix(wide_ref, a * INTER + j) for j in range(INTER)], axis=1)
        coupling_ref[a] = jnp.concatenate(two(joined), axis=0)
        return carry

    lax.fori_loop(0, LEAVES, join, 0, unroll=2)

    node = matrix(path_ref, 0)
    for i in range(1, PATH):
        node = dot(matrix(path_ref, i), node)
    nodes = [node]
    offset = 2 * LEAVES - 4
    while len(nodes) < LEAVES:
        nodes = [
            dot(node, matrix(local_ref, offset + 2 * i + k))
            for i, node in enumerate(nodes)
            for k in (0, 1)
        ]
        offset = offset - 2 * len(nodes)
    gain = DOWN ** (2 * PATH)
    for i, node in enumerate(nodes):
        columns = slice(i * LEAF, (i + 1) * LEAF)
        carried = gain * dot(node, basis_ref[:, columns])
        wide_basis_ref[:, columns] = jnp.concatenate(two(carried), axis=0)


def turned_parts(x):
    high = x.astype(bf16).astype(f32)
    stacked = jnp.concatenate([high, x - high, high, jnp.zeros_like(high)], axis=0)
    return stacked.T.astype(bf16)


def far_kernel(
    recv_ref, slots_ref, coupling_hbm, basis_hbm, wide_basis_hbm, near_hbm,
    out_hbm, coupling_ref, basis_ref, wide_basis_ref, near_ref, turned_ref,
    sems, out_sems,
):
    loads = [
        pltpu.make_async_copy(source, target, sems.at[i])
        for i, (source, target) in enumerate(
            (
                (coupling_hbm, coupling_ref),
                (basis_hbm, basis_ref),
                (wide_basis_hbm, wide_basis_ref),
                (near_hbm, near_ref),
            )
        )
    ]
    for load in loads:
        load.start()
    top = slots_ref[0, 4 * RANK :, :]
    for d in range(1, MEMBERS):
        top = top + slots_ref[d, 4 * RANK :, :]
    top = turned_parts(unfold(top))[:RHS]
    loads[0].wait()
    left = left_half((RANK, 2 * RHS))

    def far(a):
        picked = []
        for j in range(INTER):
            slot = recv_ref[0, a * INTER + j]
            use_left = (slot & 1) == 0
            rows = block(lax.shift_right_logical(slot, 1) & 3, RANK)
            picked.append(
                jnp.where(left == use_left, slots_ref[lax.shift_right_logical(slot, 3), rows, :], 0.0)
            )
        high, low = two(jnp.concatenate(picked, axis=0))
        y = jnp.dot(
            coupling_ref[a], jnp.concatenate([high, low], axis=1), preferred_element_type=f32
        )
        y = y[:RANK, : 2 * RHS] + y[:RANK, 2 * RHS :] + y[RANK:, : 2 * RHS]
        return y + swap(y)

    def turn(i, carry):
        turned_ref[i] = turned_parts(jnp.where(left, far(2 * i), far(2 * i + 1)))
        return carry

    lax.fori_loop(0, LEAVES // 2, turn, 0, unroll=8)
    for load in loads[1:]:
        load.wait()

    def finish(a, carry):
        columns = block(a, LEAF)
        basis_high, basis_low = two(basis_ref[:, columns])
        high, low = wide_basis_ref[:RANK, columns], wide_basis_ref[RANK:, columns]
        basis = jnp.concatenate(
            [basis_high, basis_high, basis_low, basis_low, high, high, low, low], axis=0
        )
        rows = turned_ref[lax.shift_right_logical(a, 1), block(a & 1, RHS), :]
        joined = jnp.concatenate([rows, top], axis=1)
        y = jnp.dot(joined, basis, preferred_element_type=f32)
        near_ref[:, columns] = near_ref[:, columns] + y
        return carry

    stores = []
    for i, part in enumerate(PARTS):
        lax.fori_loop(PART_L * i, PART_L * (i + 1), finish, 0, unroll=8)
        copy = pltpu.make_async_copy(near_ref.at[:, part], out_hbm.at[:, part], out_sems.at[i])
        copy.start()
        stores.append(copy)
    for copy in stores:
        copy.wait()


def call(kernel, name, outs, specs, scratch, kind=f32, out=vmem, aliases=None, limit=VMEM_BYTES):
    return pl.pallas_call(
        kernel,
        name=name,
        out_shape=[jax.ShapeDtypeStruct(s, kind) for s in outs],
        in_specs=specs,
        out_specs=[out] * len(outs),
        scratch_shapes=scratch,
        input_output_aliases=aliases or {},
        compiler_params=pltpu.CompilerParams(vmem_limit_bytes=limit),
        cost_estimate=pl.CostEstimate(flops=10**9, bytes_accessed=2**20, transcendentals=0),
    )


def shards(
    charges,
    coords,
    point_order,
    near_list,
    send_list,
    recv_list,
    leaf_basis,
    local_transfer,
    leaf_coupling,
    group_transfer,
    top_coupling,
):
    place = lax.axis_index("dev").astype(jnp.int32).reshape(1)
    wide = [
        pltpu.VMEM(((2 * LEAVES - 2) * RANK, LEAF), f32),
        pltpu.VMEM((8, RANK * RANK), f32),
        pltpu.VMEM((8 * RANK, LEAF), f32),
    ]
    points, first, last, coef, roots = call(
        order_kernel,
        "order",
        [
            (RHS + 8, PTS), (RHS + 8, HALO), (RHS + 8, HALO),
            (LEAVES, RANK, 2 * RHS), (GROUPS, RANK // 2, 2 * RHS),
        ],
        [smem, smem, hbm, vmem, hbm, hbm, hbm],
        [
            pltpu.VMEM((RHS, PTS), f32),
            pltpu.VMEM((RANK, PTS), f32),
            pltpu.VMEM((RHS + 8, PTS), f32),
            pltpu.VMEM((LEAVES, RANK, 2 * RHS), f32),
            pltpu.VMEM((PTS, LEAF), f32),
            pltpu.VMEM((PTS, LEAF), f32),
            pltpu.VMEM((8, PTS), f32),
            pltpu.VMEM((LEAVES // 2, RANK, 2 * RHS), f32),
            pltpu.VMEM((GROUPS, RANK // 2, 2 * RHS), f32),
            pltpu.VMEM((2 * LEAVES - 2, RANK * RANK), f32),
            pltpu.VMEM((2 * MEMBERS - 2, RANK * RANK), f32),
        ]
        + wide
        + [
            pltpu.SemaphoreType.DMA((len(PARTS) + 3,)),
            pltpu.SemaphoreType.DMA((2 * len(PARTS) + 3,)),
        ],
        out=hbm,
    )(place, point_order, charges, coords, leaf_basis, local_transfer, group_transfer)
    (sent,) = call(
        pack_kernel,
        "pack",
        [(MEMBERS, 4 * RANK + RANK // 2, 2 * RHS)],
        [smem, hbm],
        [
            pltpu.VMEM((LEAVES, RANK, 2 * RHS), f32),
            pltpu.VMEM((MEMBERS, 4 * RANK, 2 * RHS), f32),
            pltpu.SemaphoreType.DMA((5,)),
        ],
        out=hbm,
    )(send_list, coef)
    roots = lax.all_to_all(roots, "group", split_axis=0, concat_axis=0, tiled=True)
    size = lax.axis_size("group") * lax.axis_size("dev")
    up = [(i, i + 1) for i in range(size - 1)]
    back = [(i + 1, i) for i in range(size - 1)]
    before = lax.ppermute(last, ("group", "dev"), up)
    after = lax.ppermute(first, ("group", "dev"), back)
    roots, before, after = lax.optimization_barrier((roots, before, after))
    (sent,) = call(
        top_kernel,
        "top",
        [sent.shape],
        [vmem, vmem, hbm],
        [pltpu.VMEM((MEMBERS, RANK // 2, 2 * RHS), f32), pltpu.SemaphoreType.DMA],
        out=hbm,
        aliases={2: 0},
    )(roots, top_coupling, sent)
    slots = lax.all_to_all(sent, "dev", split_axis=0, concat_axis=0, tiled=True)
    (near,) = call(
        near_kernel,
        "near",
        [(RHS, PTS)],
        [smem, vmem, vmem, vmem],
        [
            pltpu.VMEM((FEATURES, PTS), bf16),
            pltpu.VMEM((WIN, FEATURES), bf16),
            pltpu.VMEM((2 * RHS, WIN), bf16),
        ],
        limit=LESS_VMEM,
    )(near_list, points, before, after)

    coupling, wide_basis = call(
        weights_kernel,
        "weights",
        [(LEAVES, 2 * RANK, INTER * RANK), (2 * RANK, PTS)],
        [smem] + [vmem] * 4,
        [pltpu.VMEM((LEAVES * INTER * RANK, LEAF), f32)] + wide,
        bf16,
        limit=LESS_VMEM,
    )(place, leaf_coupling, local_transfer, group_transfer, leaf_basis)
    (potential,) = call(
        far_kernel,
        "far",
        [(RHS, PTS)],
        [smem, vmem] + [hbm] * 4,
        [
            pltpu.VMEM((LEAVES, 2 * RANK, INTER * RANK), bf16),
            pltpu.VMEM((RANK, PTS), f32),
            pltpu.VMEM((2 * RANK, PTS), bf16),
            pltpu.VMEM((RHS, PTS), f32),
            pltpu.VMEM((LEAVES // 2, 2 * RHS, 2 * RHS), bf16),
            pltpu.SemaphoreType.DMA((4,)),
            pltpu.SemaphoreType.DMA((len(PARTS),)),
        ],
        out=hbm,
        limit=LESS_VMEM,
    )(recv_list, slots, coupling, leaf_basis, wide_basis, near)
    return potential


def solution(mesh):
    return jax.shard_map(
        shards,
        mesh=mesh,
        in_specs=(
            P(None, ("group", "dev")),
            P(None, ("group", "dev")),
            P(("group", "dev"), None),
            P(("group", "dev"), None),
            P(("group", "dev"), None),
            P(("group", "dev"), None),
            P(None, ("group", "dev")),
            P(("group", "dev"), None),
            P(("group", "dev"), None),
            P("group", None),
            P("group", None, None),
        ),
        out_specs=P(None, ("group", "dev")),
        check_vma=False,
    )
```

```python
import functools

import jax
import jax.numpy as jnp
from jax import lax
from jax.experimental import pallas as pl
from jax.experimental.pallas import tpu as pltpu
from jax.sharding import PartitionSpec as P

f32 = jnp.float32
bf16 = jnp.bfloat16
precise = lax.Precision.HIGH

LEAF = 128
RANK = 32
RHS = 64
LEAVES = 32
PTS = 4096
NEAR = 27
HALO_L = 8
HALO = HALO_L * LEAF
WIN_L = LEAVES + 2 * HALO_L
WIN = WIN_L * LEAF
INTER = 8
GROUPS = 8
MEMBERS = 32
PATH = 5
FEATURES = 48

LOG2E = 1.4426950408889634
SCALE = LOG2E * 3.0**0.5 / 0.3
FLOOR = SCALE * SCALE * 1e-6
WEIGHT = 0.1 / LOG2E
DOWN = 2.0**0.5
PART_L = HALO_L
PARTS = [slice(HALO * i, HALO * (i + 1)) for i in range(PTS // HALO)]
VMEM_BYTES = 60 * 1024 * 1024
LESS_VMEM = 50 * 1024 * 1024

vmem = pl.BlockSpec(memory_space=pltpu.VMEM)
hbm = pl.BlockSpec(memory_space=pl.ANY)
smem = pl.BlockSpec(memory_space=pltpu.SMEM)


def block(index, size):
    return pl.ds(pl.multiple_of(index * size, size), size)


def dot(a, b):
    return jnp.dot(a, b, precision=precise, preferred_element_type=f32)


def left_half(shape):
    return lax.broadcasted_iota(jnp.int32, shape, len(shape) - 1) < RHS


def swap(x):
    return pltpu.roll(x, RHS, 1)


def both(x):
    return jnp.where(left_half(x.shape), x, swap(x))


def fold(x):
    half = RANK // 2
    return jnp.where(left_half((half, 2 * RHS)), x[:half], swap(x[half:]))


def unfold(x):
    return jnp.concatenate([x, swap(x)], axis=0)


def two(x):
    high = x.astype(bf16)
    return high, (x - high.astype(f32)).astype(bf16)


def three(x):
    high = x.astype(bf16).astype(f32)
    rest = x - high
    middle = rest.astype(bf16).astype(f32)
    return high, middle, rest - middle


def spread(rows, ref, first):
    for c in range(RANK // 4):
        tile = rows[:, c * LEAF : (c + 1) * LEAF]
        for k in range(4):
            turned = tile if k == 0 else pltpu.roll(tile, LEAF - RANK * k, 1)
            ref[pl.ds(first * RANK + 4 * c + k, 8, stride=RANK), :] = turned


def matrix(ref, index):
    return ref[block(index, RANK), :RANK]


def spread_all(source_ref, ref, count):
    for first in range(0, count - 7, 8):
        spread(source_ref[first : first + 8, :], ref, first)
    if count % 8:
        spread(source_ref[count - 8 : count, :], ref, count - 8)


def spread_path(position, group_ref, rows_ref, ref):
    offset, count = 0, MEMBERS
    for i in range(8):
        if i < PATH:
            row = group_ref[pl.ds(offset + lax.shift_right_logical(position, i), 1), :]
            offset, count = offset + count, count // 2
        rows_ref[i : i + 1, :] = row
    spread(rows_ref[...], ref, 0)


def order_kernel(
    place_ref, order_ref, charges_hbm, coords_ref, basis_hbm, local_hbm, group_hbm,
    points_hbm, first_hbm, last_hbm, coef_hbm, roots_hbm,
    charges_ref, basis_ref, points_ref, coef_ref, turned_ref, rows_ref, padded_ref,
    level_ref, roots_ref, local_in_ref, group_ref, local_ref, path_in_ref, path_ref,
    sems, out_sems,
):
    loads = [
        pltpu.make_async_copy(charges_hbm.at[:, part], charges_ref.at[:, part], sems.at[i])
        for i, part in enumerate(PARTS)
    ]
    for source, target in ((basis_hbm, basis_ref), (local_hbm, local_in_ref), (group_hbm, group_ref)):
        loads.append(pltpu.make_async_copy(source, target, sems.at[len(loads)]))
    for load in loads:
        load.start()
    padded_ref[...] = jnp.zeros_like(padded_ref)
    padded_ref[0:3, :] = coords_ref[...]

    def turn(b, carry):
        columns = block(b, LEAF)
        tall = jnp.concatenate(
            [charges_ref[:, columns], padded_ref[:, columns], jnp.zeros((56, LEAF), f32)], axis=0
        )
        turned_ref[columns, :] = tall.T
        return carry

    for i in range(len(PARTS)):
        loads[i].wait()
        lax.fori_loop(PART_L * i, PART_L * (i + 1), turn, 0, unroll=8)

    def fetch(b, carry):
        for i in range(64):
            at = b * 64 + i
            rows_ref[pl.ds(at, 1), :] = turned_ref[pl.ds(order_ref[0, at], 1), :]
        return carry

    lax.fori_loop(0, PTS // 64, fetch, 0)

    def coefficient(l, carry):
        columns = block(l, LEAF)
        rows = rows_ref[columns, :]
        high, low = two(rows)
        basis_high, basis_low = two(basis_ref[:, columns])
        y = jnp.dot(
            jnp.concatenate([basis_high, basis_low], axis=0),
            jnp.concatenate([high, low], axis=1),
            preferred_element_type=f32,
        )
        y = y[:RANK, : 2 * RHS] + y[:RANK, 2 * RHS :] + y[RANK:, : 2 * RHS]
        coef_ref[l] = both(y)
        points_ref[:, columns] = rows.T[: RHS + 8]
        return carry

    for load in loads[len(PARTS) :]:
        load.wait()
    stores = []

    def store(source, target):
        copy = pltpu.make_async_copy(source, target, out_sems.at[len(stores)])
        copy.start()
        stores.append(copy)

    for i, part in enumerate(PARTS):
        lax.fori_loop(PART_L * i, PART_L * (i + 1), coefficient, 0, unroll=8)
        leaves = slice(PART_L * i, PART_L * (i + 1))
        store(coef_ref.at[leaves], coef_hbm.at[leaves])
        store(points_ref.at[:, part], points_hbm.at[:, part])
        if i == 0:
            store(points_ref.at[:, part], first_hbm)
        if i == len(PARTS) - 1:
            store(points_ref.at[:, part], last_hbm)

    spread_all(local_in_ref, local_ref, 2 * LEAVES - 2)
    spread_path(place_ref[0], group_ref, path_in_ref, path_ref)
    low, middle, high = (matrix(path_ref, i) for i in (0, 2, 4))
    path = dot(
        dot(high, matrix(path_ref, 3)), dot(middle, dot(matrix(path_ref, 1), low))
    )
    nodes = coef_ref
    offset, count = 0, LEAVES
    while count > 1:
        values = [
            dot(matrix(local_ref, offset + 2 * i), nodes[2 * i])
            + dot(matrix(local_ref, offset + 2 * i + 1), nodes[2 * i + 1])
            for i in range(count // 2)
        ]
        nodes = level_ref
        for i, value in enumerate(values):
            level_ref[i] = value
        offset, count = offset + count, count // 2
    packed = fold(dot(path, level_ref[0]))
    for g in range(GROUPS):
        roots_ref[g] = packed
    store(roots_ref, roots_hbm)
    for copy in stores:
        copy.wait()


def top_kernel(roots_ref, top_ref, sent_in_hbm, sent_hbm, tops_ref, sem):
    stacked = jnp.concatenate([unfold(roots_ref[g]) for g in range(GROUPS)], axis=0)
    packed = fold(dot(top_ref[0], stacked))
    for d in range(MEMBERS):
        tops_ref[d] = packed
    copy = pltpu.make_async_copy(tops_ref, sent_hbm.at[:, 4 * RANK :, :], sem)
    copy.start()
    copy.wait()


def pack_kernel(send_ref, coef_hbm, sent_hbm, coef_ref, sent_ref, sems):
    load = pltpu.make_async_copy(coef_hbm, coef_ref, sems.at[0])
    load.start()
    left = left_half((RANK, 2 * RHS))
    load.wait()

    def pack(d, carry):
        for q in range(4):
            one = coef_ref[send_ref[0, d * 8 + 2 * q]]
            other = coef_ref[send_ref[0, d * 8 + 2 * q + 1]]
            sent_ref[d, q * RANK : (q + 1) * RANK, :] = jnp.where(left, one, other)
        return carry

    stores = []
    for i in range(4):
        lax.fori_loop(8 * i, 8 * (i + 1), pack, 0, unroll=4)
        some = slice(8 * i, 8 * (i + 1))
        copy = pltpu.make_async_copy(
            sent_ref.at[some], sent_hbm.at[some, : 4 * RANK, :], sems.at[i + 1]
        )
        copy.start()
        stores.append(copy)
    for copy in stores:
        copy.wait()


def near_kernel(
    list_ref, points_ref, before_ref, after_ref,
    out_ref, target_ref, source_ref, weight_ref,
):
    row = lax.broadcasted_iota(jnp.int32, (8, LEAF), 0)
    zero = jnp.zeros((8, LEAF), f32)

    def prepare(w, x, own):
        columns = block(w, LEAF)
        weight_ref[:, columns] = jnp.concatenate(two(x[:RHS] * WEIGHT), axis=0)
        c = jnp.where(row < 3, (x[RHS:] - 0.5) * SCALE, 0.0)
        squares = jnp.sum(c * c, axis=0, keepdims=True) + 0.5 * FLOOR
        parts = three(jnp.broadcast_to(squares, (8, LEAF)))
        h, m, l = three(c)
        norm = jnp.where(row == 3, parts[0], jnp.where(row == 4, parts[1], parts[2]))
        is_norm = jnp.logical_and(row >= 3, row < 6)
        norm = jnp.where(is_norm, norm, 0.0)
        ones = jnp.where(is_norm, 1.0, 0.0)
        source = jnp.concatenate([h + ones, m + norm, l, h, m, h] + [zero] * 10, axis=0)
        source_ref[columns, :] = source.T[:, :FEATURES].astype(bf16)
        if own:
            target = jnp.concatenate(
                [-2.0 * h + norm, -2.0 * h + ones, -2.0 * h, -2.0 * m, -2.0 * m, -2.0 * l], axis=0
            )
            target_ref[:, block(w - HALO_L, LEAF)] = target.astype(bf16)

    def own(b, carry):
        prepare(b + HALO_L, points_ref[:, block(b, LEAF)], True)
        return carry

    lax.fori_loop(0, LEAVES, own, 0, unroll=4)
    for i in range(HALO_L):
        columns = slice(i * LEAF, (i + 1) * LEAF)
        prepare(i, before_ref[:, columns], False)
        prepare(HALO_L + LEAVES + i, after_ref[:, columns], False)

    def leaf(a, carry):
        columns = block(a, LEAF)
        target = target_ref[:, columns]
        at = [block(list_ref[a, j], LEAF) for j in range(NEAR)]
        source = jnp.concatenate([source_ref[s, :] for s in at], axis=0)
        weight = jnp.concatenate([weight_ref[:, s] for s in at], axis=1)
        squared = jnp.dot(source, target, preferred_element_type=f32)
        parts = []
        for j in range(NEAR):
            r = jnp.maximum(squared[j * LEAF : (j + 1) * LEAF], FLOOR)
            t = r * lax.rsqrt(r)
            parts.append(jnp.concatenate(two((t + LOG2E) * jnp.exp2(-t)), axis=1))
        total = jnp.dot(weight, jnp.concatenate(parts, axis=0), preferred_element_type=f32)
        out_ref[:, columns] = total[:RHS, :LEAF] + total[RHS:, :LEAF] + total[:RHS, LEAF:]
        return carry

    lax.fori_loop(0, LEAVES, leaf, 0, unroll=4)


def weights_kernel(
    place_ref, coupling_in_ref, local_in_ref, group_ref, basis_ref,
    coupling_ref, wide_basis_ref, wide_ref, local_ref, path_in_ref, path_ref,
):
    spread_all(local_in_ref, local_ref, 2 * LEAVES - 2)
    spread_path(place_ref[0], group_ref, path_in_ref, path_ref)

    def leaf(a, carry):
        spread(coupling_in_ref[block(a, INTER), :], wide_ref, a * INTER)
        return carry

    lax.fori_loop(0, LEAVES, leaf, 0, unroll=2)

    def join(a, carry):
        joined = jnp.concatenate([matrix(wide_ref, a * INTER + j) for j in range(INTER)], axis=1)
        coupling_ref[a] = jnp.concatenate(two(joined), axis=0)
        return carry

    lax.fori_loop(0, LEAVES, join, 0, unroll=2)

    node = matrix(path_ref, 0)
    for i in range(1, PATH):
        node = dot(matrix(path_ref, i), node)
    nodes = [node]
    offset = 2 * LEAVES - 4
    while len(nodes) < LEAVES:
        nodes = [
            dot(node, matrix(local_ref, offset + 2 * i + k))
            for i, node in enumerate(nodes)
            for k in (0, 1)
        ]
        offset = offset - 2 * len(nodes)
    gain = DOWN ** (2 * PATH)
    for i, node in enumerate(nodes):
        columns = slice(i * LEAF, (i + 1) * LEAF)
        carried = gain * dot(node, basis_ref[:, columns])
        wide_basis_ref[:, columns] = jnp.concatenate(two(carried), axis=0)


def turned_parts(x):
    high = x.astype(bf16).astype(f32)
    stacked = jnp.concatenate([high, x - high, high, jnp.zeros_like(high)], axis=0)
    return stacked.T.astype(bf16)


def far_kernel(
    recv_ref, slots_ref, coupling_hbm, basis_hbm, wide_basis_hbm, near_hbm,
    out_hbm, coupling_ref, basis_ref, wide_basis_ref, near_ref, turned_ref,
    sems, out_sems,
):
    loads = [
        pltpu.make_async_copy(source, target, sems.at[i])
        for i, (source, target) in enumerate(
            (
                (coupling_hbm, coupling_ref),
                (basis_hbm, basis_ref),
                (wide_basis_hbm, wide_basis_ref),
                (near_hbm, near_ref),
            )
        )
    ]
    for load in loads:
        load.start()
    top = slots_ref[0, 4 * RANK :, :]
    for d in range(1, MEMBERS):
        top = top + slots_ref[d, 4 * RANK :, :]
    top = turned_parts(unfold(top))[:RHS]
    loads[0].wait()
    left = left_half((RANK, 2 * RHS))

    def far(a):
        picked = []
        for j in range(INTER):
            slot = recv_ref[0, a * INTER + j]
            use_left = (slot & 1) == 0
            rows = block(lax.shift_right_logical(slot, 1) & 3, RANK)
            picked.append(
                jnp.where(left == use_left, slots_ref[lax.shift_right_logical(slot, 3), rows, :], 0.0)
            )
        high, low = two(jnp.concatenate(picked, axis=0))
        y = jnp.dot(
            coupling_ref[a], jnp.concatenate([high, low], axis=1), preferred_element_type=f32
        )
        y = y[:RANK, : 2 * RHS] + y[:RANK, 2 * RHS :] + y[RANK:, : 2 * RHS]
        return y + swap(y)

    def turn(i, carry):
        turned_ref[i] = turned_parts(jnp.where(left, far(2 * i), far(2 * i + 1)))
        return carry

    lax.fori_loop(0, LEAVES // 2, turn, 0, unroll=8)
    for load in loads[1:]:
        load.wait()

    def finish(a, carry):
        columns = block(a, LEAF)
        basis_high, basis_low = two(basis_ref[:, columns])
        high, low = wide_basis_ref[:RANK, columns], wide_basis_ref[RANK:, columns]
        basis = jnp.concatenate(
            [basis_high, basis_high, basis_low, basis_low, high, high, low, low], axis=0
        )
        rows = turned_ref[lax.shift_right_logical(a, 1), block(a & 1, RHS), :]
        joined = jnp.concatenate([rows, top], axis=1)
        y = jnp.dot(joined, basis, preferred_element_type=f32)
        near_ref[:, columns] = near_ref[:, columns] + y
        return carry

    stores = []
    for i, part in enumerate(PARTS):
        lax.fori_loop(PART_L * i, PART_L * (i + 1), finish, 0, unroll=8)
        copy = pltpu.make_async_copy(near_ref.at[:, part], out_hbm.at[:, part], out_sems.at[i])
        copy.start()
        stores.append(copy)
    for copy in stores:
        copy.wait()


def call(kernel, name, outs, specs, scratch, kind=f32, out=vmem, aliases=None, limit=VMEM_BYTES):
    return pl.pallas_call(
        kernel,
        name=name,
        out_shape=[jax.ShapeDtypeStruct(s, kind) for s in outs],
        in_specs=specs,
        out_specs=[out] * len(outs),
        scratch_shapes=scratch,
        input_output_aliases=aliases or {},
        compiler_params=pltpu.CompilerParams(vmem_limit_bytes=limit),
        cost_estimate=pl.CostEstimate(flops=10**9, bytes_accessed=2**20, transcendentals=0),
    )


def shards(
    charges,
    coords,
    point_order,
    near_list,
    send_list,
    recv_list,
    leaf_basis,
    local_transfer,
    leaf_coupling,
    group_transfer,
    top_coupling,
):
    place = lax.axis_index("dev").astype(jnp.int32).reshape(1)
    wide = [
        pltpu.VMEM(((2 * LEAVES - 2) * RANK, LEAF), f32),
        pltpu.VMEM((8, RANK * RANK), f32),
        pltpu.VMEM((8 * RANK, LEAF), f32),
    ]
    points, first, last, coef, roots = call(
        order_kernel,
        "order",
        [
            (RHS + 8, PTS), (RHS + 8, HALO), (RHS + 8, HALO),
            (LEAVES, RANK, 2 * RHS), (GROUPS, RANK // 2, 2 * RHS),
        ],
        [smem, smem, hbm, vmem, hbm, hbm, hbm],
        [
            pltpu.VMEM((RHS, PTS), f32),
            pltpu.VMEM((RANK, PTS), f32),
            pltpu.VMEM((RHS + 8, PTS), f32),
            pltpu.VMEM((LEAVES, RANK, 2 * RHS), f32),
            pltpu.VMEM((PTS, LEAF), f32),
            pltpu.VMEM((PTS, LEAF), f32),
            pltpu.VMEM((8, PTS), f32),
            pltpu.VMEM((LEAVES // 2, RANK, 2 * RHS), f32),
            pltpu.VMEM((GROUPS, RANK // 2, 2 * RHS), f32),
            pltpu.VMEM((2 * LEAVES - 2, RANK * RANK), f32),
            pltpu.VMEM((2 * MEMBERS - 2, RANK * RANK), f32),
        ]
        + wide
        + [
            pltpu.SemaphoreType.DMA((len(PARTS) + 3,)),
            pltpu.SemaphoreType.DMA((2 * len(PARTS) + 3,)),
        ],
        out=hbm,
    )(place, point_order, charges, coords, leaf_basis, local_transfer, group_transfer)
    (sent,) = call(
        pack_kernel,
        "pack",
        [(MEMBERS, 4 * RANK + RANK // 2, 2 * RHS)],
        [smem, hbm],
        [
            pltpu.VMEM((LEAVES, RANK, 2 * RHS), f32),
            pltpu.VMEM((MEMBERS, 4 * RANK, 2 * RHS), f32),
            pltpu.SemaphoreType.DMA((5,)),
        ],
        out=hbm,
    )(send_list, coef)
    roots = lax.all_to_all(roots, "group", split_axis=0, concat_axis=0, tiled=True)
    size = lax.axis_size("group") * lax.axis_size("dev")
    up = [(i, i + 1) for i in range(size - 1)]
    back = [(i + 1, i) for i in range(size - 1)]
    before = lax.ppermute(last, ("group", "dev"), up)
    after = lax.ppermute(first, ("group", "dev"), back)
    roots, before, after = lax.optimization_barrier((roots, before, after))
    (sent,) = call(
        top_kernel,
        "top",
        [sent.shape],
        [vmem, vmem, hbm],
        [pltpu.VMEM((MEMBERS, RANK // 2, 2 * RHS), f32), pltpu.SemaphoreType.DMA],
        out=hbm,
        aliases={2: 0},
    )(roots, top_coupling, sent)
    slots = lax.all_to_all(sent, "dev", split_axis=0, concat_axis=0, tiled=True)
    (near,) = call(
        near_kernel,
        "near",
        [(RHS, PTS)],
        [smem, vmem, vmem, vmem],
        [
            pltpu.VMEM((FEATURES, PTS), bf16),
            pltpu.VMEM((WIN, FEATURES), bf16),
            pltpu.VMEM((2 * RHS, WIN), bf16),
        ],
        limit=LESS_VMEM,
    )(near_list, points, before, after)

    coupling, wide_basis = call(
        weights_kernel,
        "weights",
        [(LEAVES, 2 * RANK, INTER * RANK), (2 * RANK, PTS)],
        [smem] + [vmem] * 4,
        [pltpu.VMEM((LEAVES * INTER * RANK, LEAF), f32)] + wide,
        bf16,
        limit=LESS_VMEM,
    )(place, leaf_coupling, local_transfer, group_transfer, leaf_basis)
    (potential,) = call(
        far_kernel,
        "far",
        [(RHS, PTS)],
        [smem, vmem] + [hbm] * 4,
        [
            pltpu.VMEM((LEAVES, 2 * RANK, INTER * RANK), bf16),
            pltpu.VMEM((RANK, PTS), f32),
            pltpu.VMEM((2 * RANK, PTS), bf16),
            pltpu.VMEM((RHS, PTS), f32),
            pltpu.VMEM((LEAVES // 2, 2 * RHS, 2 * RHS), bf16),
            pltpu.SemaphoreType.DMA((4,)),
            pltpu.SemaphoreType.DMA((len(PARTS),)),
        ],
        out=hbm,
        limit=LESS_VMEM,
    )(recv_list, slots, coupling, leaf_basis, wide_basis, near)
    return potential


def solution(mesh):
    return jax.shard_map(
        shards,
        mesh=mesh,
        in_specs=(
            P(None, ("group", "dev")),
            P(None, ("group", "dev")),
            P(("group", "dev"), None),
            P(("group", "dev"), None),
            P(("group", "dev"), None),
            P(("group", "dev"), None),
            P(None, ("group", "dev")),
            P(("group", "dev"), None),
            P(("group", "dev"), None),
            P("group", None),
            P("group", None, None),
        ),
        out_specs=P(None, ("group", "dev")),
        check_vma=False,
    )
```

```python
import functools

import jax
import jax.numpy as jnp
from jax import lax
from jax.experimental import pallas as pl
from jax.experimental.pallas import tpu as pltpu
from jax.sharding import PartitionSpec as P

f32 = jnp.float32
bf16 = jnp.bfloat16
precise = lax.Precision.HIGHEST

LEAF = 128
RANK = 32
RHS = 64
LEAVES = 32
PTS = 4096
NEAR = 27
HALO_L = 8
HALO = HALO_L * LEAF
WIN_L = LEAVES + 2 * HALO_L
WIN = WIN_L * LEAF
INTER = 8
GROUPS = 8
MEMBERS = 32
PATH = 5
FEATURES = 48

LOG2E = 1.4426950408889634
SCALE = LOG2E * 3.0**0.5 / 0.3
FLOOR = SCALE * SCALE * 1e-6
WEIGHT = 0.1 / LOG2E
DOWN = 2.0**0.5
PART_L = HALO_L
PARTS = [slice(HALO * i, HALO * (i + 1)) for i in range(PTS // HALO)]
VMEM_BYTES = 60 * 1024 * 1024
LESS_VMEM = 50 * 1024 * 1024

vmem = pl.BlockSpec(memory_space=pltpu.VMEM)
hbm = pl.BlockSpec(memory_space=pl.ANY)
smem = pl.BlockSpec(memory_space=pltpu.SMEM)


def block(index, size):
    return pl.ds(pl.multiple_of(index * size, size), size)


def dot(a, b):
    return jnp.dot(a, b, precision=precise, preferred_element_type=f32)


def left_half(shape):
    return lax.broadcasted_iota(jnp.int32, shape, len(shape) - 1) < RHS


def swap(x):
    return pltpu.roll(x, RHS, 1)


def both(x):
    return jnp.where(left_half(x.shape), x, swap(x))


def fold(x):
    half = RANK // 2
    return jnp.where(left_half((half, 2 * RHS)), x[:half], swap(x[half:]))


def unfold(x):
    return jnp.concatenate([x, swap(x)], axis=0)


def two(x):
    high = x.astype(bf16)
    return high, (x - high.astype(f32)).astype(bf16)


def three(x):
    high = x.astype(bf16).astype(f32)
    rest = x - high
    middle = rest.astype(bf16).astype(f32)
    return high, middle, rest - middle


def spread(rows, ref, first):
    for c in range(RANK // 4):
        tile = rows[:, c * LEAF : (c + 1) * LEAF]
        for k in range(4):
            turned = tile if k == 0 else pltpu.roll(tile, LEAF - RANK * k, 1)
            ref[pl.ds(first * RANK + 4 * c + k, 8, stride=RANK), :] = turned


def matrix(ref, index):
    return ref[block(index, RANK), :RANK]


def spread_all(source_ref, ref, count):
    for first in range(0, count - 7, 8):
        spread(source_ref[first : first + 8, :], ref, first)
    if count % 8:
        spread(source_ref[count - 8 : count, :], ref, count - 8)


def spread_path(position, group_ref, rows_ref, ref):
    offset, count = 0, MEMBERS
    for i in range(8):
        if i < PATH:
            row = group_ref[pl.ds(offset + lax.shift_right_logical(position, i), 1), :]
            offset, count = offset + count, count // 2
        rows_ref[i : i + 1, :] = row
    spread(rows_ref[...], ref, 0)


def order_kernel(
    place_ref, order_ref, charges_hbm, coords_ref, basis_hbm, local_hbm, group_hbm,
    points_hbm, first_hbm, last_hbm, coef_hbm, roots_hbm,
    charges_ref, basis_ref, points_ref, coef_ref, turned_ref, rows_ref, padded_ref,
    level_ref, roots_ref, local_in_ref, group_ref, local_ref, path_in_ref, path_ref,
    sems, out_sems,
):
    loads = [
        pltpu.make_async_copy(charges_hbm.at[:, part], charges_ref.at[:, part], sems.at[i])
        for i, part in enumerate(PARTS)
    ]
    for source, target in ((basis_hbm, basis_ref), (local_hbm, local_in_ref), (group_hbm, group_ref)):
        loads.append(pltpu.make_async_copy(source, target, sems.at[len(loads)]))
    for load in loads:
        load.start()
    padded_ref[...] = jnp.zeros_like(padded_ref)
    padded_ref[0:3, :] = coords_ref[...]

    def turn(b, carry):
        columns = block(b, LEAF)
        tall = jnp.concatenate(
            [charges_ref[:, columns], padded_ref[:, columns], jnp.zeros((56, LEAF), f32)], axis=0
        )
        turned_ref[columns, :] = tall.T
        return carry

    for i in range(len(PARTS)):
        loads[i].wait()
        lax.fori_loop(PART_L * i, PART_L * (i + 1), turn, 0, unroll=8)

    def fetch(b, carry):
        for i in range(64):
            at = b * 64 + i
            rows_ref[pl.ds(at, 1), :] = turned_ref[pl.ds(order_ref[0, at], 1), :]
        return carry

    lax.fori_loop(0, PTS // 64, fetch, 0)

    def coefficient(l, carry):
        columns = block(l, LEAF)
        rows = rows_ref[columns, :]
        high, low = two(rows)
        basis_high, basis_low = two(basis_ref[:, columns])
        y = jnp.dot(
            jnp.concatenate([basis_high, basis_low], axis=0),
            jnp.concatenate([high, low], axis=1),
            preferred_element_type=f32,
        )
        y = y[:RANK, : 2 * RHS] + y[:RANK, 2 * RHS :] + y[RANK:, : 2 * RHS]
        coef_ref[l] = both(y)
        points_ref[:, columns] = rows.T[: RHS + 8]
        return carry

    for load in loads[len(PARTS) :]:
        load.wait()
    stores = []

    def store(source, target):
        copy = pltpu.make_async_copy(source, target, out_sems.at[len(stores)])
        copy.start()
        stores.append(copy)

    for i, part in enumerate(PARTS):
        lax.fori_loop(PART_L * i, PART_L * (i + 1), coefficient, 0, unroll=8)
        leaves = slice(PART_L * i, PART_L * (i + 1))
        store(coef_ref.at[leaves], coef_hbm.at[leaves])
        store(points_ref.at[:, part], points_hbm.at[:, part])
        if i == 0:
            store(points_ref.at[:, part], first_hbm)
        if i == len(PARTS) - 1:
            store(points_ref.at[:, part], last_hbm)

    spread_all(local_in_ref, local_ref, 2 * LEAVES - 2)
    spread_path(place_ref[0], group_ref, path_in_ref, path_ref)
    low, middle, high = (matrix(path_ref, i) for i in (0, 2, 4))
    path = dot(
        dot(high, matrix(path_ref, 3)), dot(middle, dot(matrix(path_ref, 1), low))
    )
    nodes = coef_ref
    offset, count = 0, LEAVES
    while count > 1:
        values = [
            dot(matrix(local_ref, offset + 2 * i), nodes[2 * i])
            + dot(matrix(local_ref, offset + 2 * i + 1), nodes[2 * i + 1])
            for i in range(count // 2)
        ]
        nodes = level_ref
        for i, value in enumerate(values):
            level_ref[i] = value
        offset, count = offset + count, count // 2
    packed = fold(dot(path, level_ref[0]))
    for g in range(GROUPS):
        roots_ref[g] = packed
    store(roots_ref, roots_hbm)
    for copy in stores:
        copy.wait()


def top_kernel(roots_ref, top_ref, sent_in_hbm, sent_hbm, tops_ref, sem):
    stacked = jnp.concatenate([unfold(roots_ref[g]) for g in range(GROUPS)], axis=0)
    packed = fold(dot(top_ref[0], stacked))
    for d in range(MEMBERS):
        tops_ref[d] = packed
    copy = pltpu.make_async_copy(tops_ref, sent_hbm.at[:, 4 * RANK :, :], sem)
    copy.start()
    copy.wait()


def pack_kernel(send_ref, coef_hbm, sent_hbm, coef_ref, sent_ref, sems):
    load = pltpu.make_async_copy(coef_hbm, coef_ref, sems.at[0])
    load.start()
    left = left_half((RANK, 2 * RHS))
    load.wait()

    def pack(d, carry):
        for q in range(4):
            one = coef_ref[send_ref[0, d * 8 + 2 * q]]
            other = coef_ref[send_ref[0, d * 8 + 2 * q + 1]]
            sent_ref[d, q * RANK : (q + 1) * RANK, :] = jnp.where(left, one, other)
        return carry

    stores = []
    for i in range(4):
        lax.fori_loop(8 * i, 8 * (i + 1), pack, 0, unroll=4)
        some = slice(8 * i, 8 * (i + 1))
        copy = pltpu.make_async_copy(
            sent_ref.at[some], sent_hbm.at[some, : 4 * RANK, :], sems.at[i + 1]
        )
        copy.start()
        stores.append(copy)
    for copy in stores:
        copy.wait()


def near_kernel(
    list_ref, points_ref, before_ref, after_ref,
    out_ref, target_ref, source_ref, weight_ref,
):
    row = lax.broadcasted_iota(jnp.int32, (8, LEAF), 0)
    zero = jnp.zeros((8, LEAF), f32)

    def prepare(w, x, own):
        columns = block(w, LEAF)
        weight_ref[:, columns] = jnp.concatenate(two(x[:RHS] * WEIGHT), axis=0)
        c = jnp.where(row < 3, (x[RHS:] - 0.5) * SCALE, 0.0)
        squares = jnp.sum(c * c, axis=0, keepdims=True) + 0.5 * FLOOR
        parts = three(jnp.broadcast_to(squares, (8, LEAF)))
        h, m, l = three(c)
        norm = jnp.where(row == 3, parts[0], jnp.where(row == 4, parts[1], parts[2]))
        is_norm = jnp.logical_and(row >= 3, row < 6)
        norm = jnp.where(is_norm, norm, 0.0)
        ones = jnp.where(is_norm, 1.0, 0.0)
        source = jnp.concatenate([h + ones, m + norm, l, h, m, h] + [zero] * 10, axis=0)
        source_ref[columns, :] = source.T[:, :FEATURES].astype(bf16)
        if own:
            target = jnp.concatenate(
                [-2.0 * h + norm, -2.0 * h + ones, -2.0 * h, -2.0 * m, -2.0 * m, -2.0 * l], axis=0
            )
            target_ref[:, block(w - HALO_L, LEAF)] = target.astype(bf16)

    def own(b, carry):
        prepare(b + HALO_L, points_ref[:, block(b, LEAF)], True)
        return carry

    lax.fori_loop(0, LEAVES, own, 0, unroll=4)
    for i in range(HALO_L):
        columns = slice(i * LEAF, (i + 1) * LEAF)
        prepare(i, before_ref[:, columns], False)
        prepare(HALO_L + LEAVES + i, after_ref[:, columns], False)

    def leaf(a, carry):
        columns = block(a, LEAF)
        target = target_ref[:, columns]
        at = [block(list_ref[a, j], LEAF) for j in range(NEAR)]
        source = jnp.concatenate([source_ref[s, :] for s in at], axis=0)
        weight = jnp.concatenate([weight_ref[:, s] for s in at], axis=1)
        squared = jnp.dot(source, target, preferred_element_type=f32)
        parts = []
        for j in range(NEAR):
            r = jnp.maximum(squared[j * LEAF : (j + 1) * LEAF], FLOOR)
            t = r * lax.rsqrt(r)
            parts.append(jnp.concatenate(two((t + LOG2E) * jnp.exp2(-t)), axis=1))
        total = jnp.dot(weight, jnp.concatenate(parts, axis=0), preferred_element_type=f32)
        out_ref[:, columns] = total[:RHS, :LEAF] + total[RHS:, :LEAF] + total[:RHS, LEAF:]
        return carry

    lax.fori_loop(0, LEAVES, leaf, 0, unroll=4)


def weights_kernel(
    place_ref, coupling_in_ref, local_in_ref, group_ref, basis_ref,
    coupling_ref, wide_basis_ref, wide_ref, local_ref, path_in_ref, path_ref,
):
    spread_all(local_in_ref, local_ref, 2 * LEAVES - 2)
    spread_path(place_ref[0], group_ref, path_in_ref, path_ref)

    def leaf(a, carry):
        spread(coupling_in_ref[block(a, INTER), :], wide_ref, a * INTER)
        return carry

    lax.fori_loop(0, LEAVES, leaf, 0, unroll=2)

    def join(a, carry):
        joined = jnp.concatenate([matrix(wide_ref, a * INTER + j) for j in range(INTER)], axis=1)
        coupling_ref[a] = jnp.concatenate(two(joined), axis=0)
        return carry

    lax.fori_loop(0, LEAVES, join, 0, unroll=2)

    node = matrix(path_ref, 0)
    for i in range(1, PATH):
        node = dot(matrix(path_ref, i), node)
    nodes = [node]
    offset = 2 * LEAVES - 4
    while len(nodes) < LEAVES:
        nodes = [
            dot(node, matrix(local_ref, offset + 2 * i + k))
            for i, node in enumerate(nodes)
            for k in (0, 1)
        ]
        offset = offset - 2 * len(nodes)
    gain = DOWN ** (2 * PATH)
    for i, node in enumerate(nodes):
        columns = slice(i * LEAF, (i + 1) * LEAF)
        carried = gain * dot(node, basis_ref[:, columns])
        wide_basis_ref[:, columns] = jnp.concatenate(two(carried), axis=0)


def turned_parts(x):
    high = x.astype(bf16).astype(f32)
    stacked = jnp.concatenate([high, x - high, high, jnp.zeros_like(high)], axis=0)
    return stacked.T.astype(bf16)


def far_kernel(
    recv_ref, slots_ref, coupling_hbm, basis_hbm, wide_basis_hbm, near_hbm,
    out_hbm, coupling_ref, basis_ref, wide_basis_ref, near_ref, turned_ref,
    sems, out_sems,
):
    loads = [
        pltpu.make_async_copy(source, target, sems.at[i])
        for i, (source, target) in enumerate(
            (
                (coupling_hbm, coupling_ref),
                (basis_hbm, basis_ref),
                (wide_basis_hbm, wide_basis_ref),
                (near_hbm, near_ref),
            )
        )
    ]
    for load in loads:
        load.start()
    top = slots_ref[0, 4 * RANK :, :]
    for d in range(1, MEMBERS):
        top = top + slots_ref[d, 4 * RANK :, :]
    top = turned_parts(unfold(top))[:RHS]
    loads[0].wait()
    left = left_half((RANK, 2 * RHS))

    def far(a):
        picked = []
        for j in range(INTER):
            slot = recv_ref[0, a * INTER + j]
            use_left = (slot & 1) == 0
            rows = block(lax.shift_right_logical(slot, 1) & 3, RANK)
            picked.append(
                jnp.where(left == use_left, slots_ref[lax.shift_right_logical(slot, 3), rows, :], 0.0)
            )
        high, low = two(jnp.concatenate(picked, axis=0))
        y = jnp.dot(
            coupling_ref[a], jnp.concatenate([high, low], axis=1), preferred_element_type=f32
        )
        y = y[:RANK, : 2 * RHS] + y[:RANK, 2 * RHS :] + y[RANK:, : 2 * RHS]
        return y + swap(y)

    def turn(i, carry):
        turned_ref[i] = turned_parts(jnp.where(left, far(2 * i), far(2 * i + 1)))
        return carry

    lax.fori_loop(0, LEAVES // 2, turn, 0, unroll=8)
    for load in loads[1:]:
        load.wait()

    def finish(a, carry):
        columns = block(a, LEAF)
        basis_high, basis_low = two(basis_ref[:, columns])
        high, low = wide_basis_ref[:RANK, columns], wide_basis_ref[RANK:, columns]
        basis = jnp.concatenate(
            [basis_high, basis_high, basis_low, basis_low, high, high, low, low], axis=0
        )
        rows = turned_ref[lax.shift_right_logical(a, 1), block(a & 1, RHS), :]
        joined = jnp.concatenate([rows, top], axis=1)
        y = jnp.dot(joined, basis, preferred_element_type=f32)
        near_ref[:, columns] = near_ref[:, columns] + y
        return carry

    stores = []
    for i, part in enumerate(PARTS):
        lax.fori_loop(PART_L * i, PART_L * (i + 1), finish, 0, unroll=8)
        copy = pltpu.make_async_copy(near_ref.at[:, part], out_hbm.at[:, part], out_sems.at[i])
        copy.start()
        stores.append(copy)
    for copy in stores:
        copy.wait()


def call(kernel, name, outs, specs, scratch, kind=f32, out=vmem, aliases=None, limit=VMEM_BYTES):
    return pl.pallas_call(
        kernel,
        name=name,
        out_shape=[jax.ShapeDtypeStruct(s, kind) for s in outs],
        in_specs=specs,
        out_specs=[out] * len(outs),
        scratch_shapes=scratch,
        input_output_aliases=aliases or {},
        compiler_params=pltpu.CompilerParams(vmem_limit_bytes=limit),
        cost_estimate=pl.CostEstimate(flops=10**9, bytes_accessed=2**20, transcendentals=0),
    )


def shards(
    charges,
    coords,
    point_order,
    near_list,
    send_list,
    recv_list,
    leaf_basis,
    local_transfer,
    leaf_coupling,
    group_transfer,
    top_coupling,
):
    place = lax.axis_index("dev").astype(jnp.int32).reshape(1)
    wide = [
        pltpu.VMEM(((2 * LEAVES - 2) * RANK, LEAF), f32),
        pltpu.VMEM((8, RANK * RANK), f32),
        pltpu.VMEM((8 * RANK, LEAF), f32),
    ]
    points, first, last, coef, roots = call(
        order_kernel,
        "order",
        [
            (RHS + 8, PTS), (RHS + 8, HALO), (RHS + 8, HALO),
            (LEAVES, RANK, 2 * RHS), (GROUPS, RANK // 2, 2 * RHS),
        ],
        [smem, smem, hbm, vmem, hbm, hbm, hbm],
        [
            pltpu.VMEM((RHS, PTS), f32),
            pltpu.VMEM((RANK, PTS), f32),
            pltpu.VMEM((RHS + 8, PTS), f32),
            pltpu.VMEM((LEAVES, RANK, 2 * RHS), f32),
            pltpu.VMEM((PTS, LEAF), f32),
            pltpu.VMEM((PTS, LEAF), f32),
            pltpu.VMEM((8, PTS), f32),
            pltpu.VMEM((LEAVES // 2, RANK, 2 * RHS), f32),
            pltpu.VMEM((GROUPS, RANK // 2, 2 * RHS), f32),
            pltpu.VMEM((2 * LEAVES - 2, RANK * RANK), f32),
            pltpu.VMEM((2 * MEMBERS - 2, RANK * RANK), f32),
        ]
        + wide
        + [
            pltpu.SemaphoreType.DMA((len(PARTS) + 3,)),
            pltpu.SemaphoreType.DMA((2 * len(PARTS) + 3,)),
        ],
        out=hbm,
    )(place, point_order, charges, coords, leaf_basis, local_transfer, group_transfer)
    (sent,) = call(
        pack_kernel,
        "pack",
        [(MEMBERS, 4 * RANK + RANK // 2, 2 * RHS)],
        [smem, hbm],
        [
            pltpu.VMEM((LEAVES, RANK, 2 * RHS), f32),
            pltpu.VMEM((MEMBERS, 4 * RANK, 2 * RHS), f32),
            pltpu.SemaphoreType.DMA((5,)),
        ],
        out=hbm,
    )(send_list, coef)
    roots = lax.all_to_all(roots, "group", split_axis=0, concat_axis=0, tiled=True)
    size = lax.axis_size("group") * lax.axis_size("dev")
    up = [(i, i + 1) for i in range(size - 1)]
    back = [(i + 1, i) for i in range(size - 1)]
    before = lax.ppermute(last, ("group", "dev"), up)
    after = lax.ppermute(first, ("group", "dev"), back)
    roots, before, after = lax.optimization_barrier((roots, before, after))
    (sent,) = call(
        top_kernel,
        "top",
        [sent.shape],
        [vmem, vmem, hbm],
        [pltpu.VMEM((MEMBERS, RANK // 2, 2 * RHS), f32), pltpu.SemaphoreType.DMA],
        out=hbm,
        aliases={2: 0},
    )(roots, top_coupling, sent)
    slots = lax.all_to_all(sent, "dev", split_axis=0, concat_axis=0, tiled=True)
    (near,) = call(
        near_kernel,
        "near",
        [(RHS, PTS)],
        [smem, vmem, vmem, vmem],
        [
            pltpu.VMEM((FEATURES, PTS), bf16),
            pltpu.VMEM((WIN, FEATURES), bf16),
            pltpu.VMEM((2 * RHS, WIN), bf16),
        ],
        limit=LESS_VMEM,
    )(near_list, points, before, after)

    coupling, wide_basis = call(
        weights_kernel,
        "weights",
        [(LEAVES, 2 * RANK, INTER * RANK), (2 * RANK, PTS)],
        [smem] + [vmem] * 4,
        [pltpu.VMEM((LEAVES * INTER * RANK, LEAF), f32)] + wide,
        bf16,
        limit=LESS_VMEM,
    )(place, leaf_coupling, local_transfer, group_transfer, leaf_basis)
    (potential,) = call(
        far_kernel,
        "far",
        [(RHS, PTS)],
        [smem, vmem] + [hbm] * 4,
        [
            pltpu.VMEM((LEAVES, 2 * RANK, INTER * RANK), bf16),
            pltpu.VMEM((RANK, PTS), f32),
            pltpu.VMEM((2 * RANK, PTS), bf16),
            pltpu.VMEM((RHS, PTS), f32),
            pltpu.VMEM((LEAVES // 2, 2 * RHS, 2 * RHS), bf16),
            pltpu.SemaphoreType.DMA((4,)),
            pltpu.SemaphoreType.DMA((len(PARTS),)),
        ],
        out=hbm,
        limit=LESS_VMEM,
    )(recv_list, slots, coupling, leaf_basis, wide_basis, near)
    return potential


def solution(mesh):
    return jax.shard_map(
        shards,
        mesh=mesh,
        in_specs=(
            P(None, ("group", "dev")),
            P(None, ("group", "dev")),
            P(("group", "dev"), None),
            P(("group", "dev"), None),
            P(("group", "dev"), None),
            P(("group", "dev"), None),
            P(None, ("group", "dev")),
            P(("group", "dev"), None),
            P(("group", "dev"), None),
            P("group", None),
            P("group", None, None),
        ),
        out_specs=P(None, ("group", "dev")),
        check_vma=False,
    )
```

```python
import functools

import jax
import jax.numpy as jnp
from jax import lax
from jax.experimental import pallas as pl
from jax.experimental.pallas import tpu as pltpu
from jax.sharding import PartitionSpec as P

f32 = jnp.float32
bf16 = jnp.bfloat16
precise = lax.Precision.HIGHEST

LEAF = 128
RANK = 32
RHS = 64
LEAVES = 32
PTS = 4096
NEAR = 27
HALO_L = 8
HALO = HALO_L * LEAF
WIN_L = LEAVES + 2 * HALO_L
WIN = WIN_L * LEAF
INTER = 8
GROUPS = 8
MEMBERS = 32
PATH = 5
FEATURES = 48

LOG2E = 1.4426950408889634
SCALE = LOG2E * 3.0**0.5 / 0.3
FLOOR = SCALE * SCALE * 1e-6
WEIGHT = 0.1 / LOG2E
DOWN = 2.0**0.5
PART_L = HALO_L
PARTS = [slice(HALO * i, HALO * (i + 1)) for i in range(PTS // HALO)]
VMEM_BYTES = 60 * 1024 * 1024
LESS_VMEM = 50 * 1024 * 1024

vmem = pl.BlockSpec(memory_space=pltpu.VMEM)
hbm = pl.BlockSpec(memory_space=pl.ANY)
smem = pl.BlockSpec(memory_space=pltpu.SMEM)


def block(index, size):
    return pl.ds(pl.multiple_of(index * size, size), size)


def dot(a, b):
    return jnp.dot(a, b, precision=precise, preferred_element_type=f32)


def left_half(shape):
    return lax.broadcasted_iota(jnp.int32, shape, len(shape) - 1) < RHS


def swap(x):
    return pltpu.roll(x, RHS, 1)


def both(x):
    return jnp.where(left_half(x.shape), x, swap(x))


def fold(x):
    half = RANK // 2
    return jnp.where(left_half((half, 2 * RHS)), x[:half], swap(x[half:]))


def unfold(x):
    return jnp.concatenate([x, swap(x)], axis=0)


def two(x):
    high = x.astype(bf16)
    return high, (x - high.astype(f32)).astype(bf16)


def three(x):
    high = x.astype(bf16).astype(f32)
    rest = x - high
    middle = rest.astype(bf16).astype(f32)
    return high, middle, rest - middle


def spread(rows, ref, first):
    for c in range(RANK // 4):
        tile = rows[:, c * LEAF : (c + 1) * LEAF]
        for k in range(4):
            turned = tile if k == 0 else pltpu.roll(tile, LEAF - RANK * k, 1)
            ref[pl.ds(first * RANK + 4 * c + k, 8, stride=RANK), :] = turned


def matrix(ref, index):
    return ref[block(index, RANK), :RANK]


def spread_all(source_ref, ref, count):
    for first in range(0, count - 7, 8):
        spread(source_ref[first : first + 8, :], ref, first)
    if count % 8:
        spread(source_ref[count - 8 : count, :], ref, count - 8)


def spread_path(position, group_ref, rows_ref, ref):
    offset, count = 0, MEMBERS
    for i in range(8):
        if i < PATH:
            row = group_ref[pl.ds(offset + lax.shift_right_logical(position, i), 1), :]
            offset, count = offset + count, count // 2
        rows_ref[i : i + 1, :] = row
    spread(rows_ref[...], ref, 0)


def order_kernel(
    place_ref, order_ref, charges_hbm, coords_ref, basis_hbm, local_hbm, group_hbm,
    points_hbm, first_hbm, last_hbm, coef_hbm, roots_hbm,
    charges_ref, basis_ref, points_ref, coef_ref, turned_ref, rows_ref, padded_ref,
    level_ref, roots_ref, local_in_ref, group_ref, local_ref, path_in_ref, path_ref,
    sems, out_sems,
):
    loads = [
        pltpu.make_async_copy(charges_hbm.at[:, part], charges_ref.at[:, part], sems.at[i])
        for i, part in enumerate(PARTS)
    ]
    for source, target in ((basis_hbm, basis_ref), (local_hbm, local_in_ref), (group_hbm, group_ref)):
        loads.append(pltpu.make_async_copy(source, target, sems.at[len(loads)]))
    for load in loads:
        load.start()
    padded_ref[...] = jnp.zeros_like(padded_ref)
    padded_ref[0:3, :] = coords_ref[...]

    def turn(b, carry):
        columns = block(b, LEAF)
        tall = jnp.concatenate(
            [charges_ref[:, columns], padded_ref[:, columns], jnp.zeros((56, LEAF), f32)], axis=0
        )
        turned_ref[columns, :] = tall.T
        return carry

    for i in range(len(PARTS)):
        loads[i].wait()
        lax.fori_loop(PART_L * i, PART_L * (i + 1), turn, 0, unroll=8)

    def fetch(b, carry):
        for i in range(128):
            at = b * 128 + i
            rows_ref[pl.ds(at, 1), :] = turned_ref[pl.ds(order_ref[0, at], 1), :]
        return carry

    lax.fori_loop(0, PTS // 128, fetch, 0)

    def coefficient(l, carry):
        columns = block(l, LEAF)
        rows = rows_ref[columns, :]
        high, low = two(rows)
        basis_high, basis_low = two(basis_ref[:, columns])
        y = jnp.dot(
            jnp.concatenate([basis_high, basis_low], axis=0),
            jnp.concatenate([high, low], axis=1),
            preferred_element_type=f32,
        )
        y = y[:RANK, : 2 * RHS] + y[:RANK, 2 * RHS :] + y[RANK:, : 2 * RHS]
        coef_ref[l] = both(y)
        points_ref[:, columns] = rows.T[: RHS + 8]
        return carry

    for load in loads[len(PARTS) :]:
        load.wait()
    stores = []

    def store(source, target):
        copy = pltpu.make_async_copy(source, target, out_sems.at[len(stores)])
        copy.start()
        stores.append(copy)

    for i, part in enumerate(PARTS):
        lax.fori_loop(PART_L * i, PART_L * (i + 1), coefficient, 0, unroll=8)
        leaves = slice(PART_L * i, PART_L * (i + 1))
        store(coef_ref.at[leaves], coef_hbm.at[leaves])
        store(points_ref.at[:, part], points_hbm.at[:, part])
        if i == 0:
            store(points_ref.at[:, part], first_hbm)
        if i == len(PARTS) - 1:
            store(points_ref.at[:, part], last_hbm)

    spread_all(local_in_ref, local_ref, 2 * LEAVES - 2)
    spread_path(place_ref[0], group_ref, path_in_ref, path_ref)
    low, middle, high = (matrix(path_ref, i) for i in (0, 2, 4))
    path = dot(
        dot(high, matrix(path_ref, 3)), dot(middle, dot(matrix(path_ref, 1), low))
    )
    nodes = coef_ref
    offset, count = 0, LEAVES
    while count > 1:
        values = [
            dot(matrix(local_ref, offset + 2 * i), nodes[2 * i])
            + dot(matrix(local_ref, offset + 2 * i + 1), nodes[2 * i + 1])
            for i in range(count // 2)
        ]
        nodes = level_ref
        for i, value in enumerate(values):
            level_ref[i] = value
        offset, count = offset + count, count // 2
    packed = fold(dot(path, level_ref[0]))
    for g in range(GROUPS):
        roots_ref[g] = packed
    store(roots_ref, roots_hbm)
    for copy in stores:
        copy.wait()


def top_kernel(roots_ref, top_ref, sent_in_hbm, sent_hbm, tops_ref, sem):
    stacked = jnp.concatenate([unfold(roots_ref[g]) for g in range(GROUPS)], axis=0)
    packed = fold(dot(top_ref[0], stacked))
    for d in range(MEMBERS):
        tops_ref[d] = packed
    copy = pltpu.make_async_copy(tops_ref, sent_hbm.at[:, 4 * RANK :, :], sem)
    copy.start()
    copy.wait()


def pack_kernel(send_ref, coef_hbm, sent_hbm, coef_ref, sent_ref, sems):
    load = pltpu.make_async_copy(coef_hbm, coef_ref, sems.at[0])
    load.start()
    left = left_half((RANK, 2 * RHS))
    load.wait()

    def pack(d, carry):
        for q in range(4):
            one = coef_ref[send_ref[0, d * 8 + 2 * q]]
            other = coef_ref[send_ref[0, d * 8 + 2 * q + 1]]
            sent_ref[d, q * RANK : (q + 1) * RANK, :] = jnp.where(left, one, other)
        return carry

    stores = []
    for i in range(4):
        lax.fori_loop(8 * i, 8 * (i + 1), pack, 0, unroll=4)
        some = slice(8 * i, 8 * (i + 1))
        copy = pltpu.make_async_copy(
            sent_ref.at[some], sent_hbm.at[some, : 4 * RANK, :], sems.at[i + 1]
        )
        copy.start()
        stores.append(copy)
    for copy in stores:
        copy.wait()


def near_kernel(
    list_ref, points_ref, before_ref, after_ref,
    out_ref, target_ref, source_ref, weight_ref,
):
    row = lax.broadcasted_iota(jnp.int32, (8, LEAF), 0)
    zero = jnp.zeros((8, LEAF), f32)

    def prepare(w, x, own):
        columns = block(w, LEAF)
        weight_ref[:, columns] = jnp.concatenate(two(x[:RHS] * WEIGHT), axis=0)
        c = jnp.where(row < 3, (x[RHS:] - 0.5) * SCALE, 0.0)
        squares = jnp.sum(c * c, axis=0, keepdims=True) + 0.5 * FLOOR
        parts = three(jnp.broadcast_to(squares, (8, LEAF)))
        h, m, l = three(c)
        norm = jnp.where(row == 3, parts[0], jnp.where(row == 4, parts[1], parts[2]))
        is_norm = jnp.logical_and(row >= 3, row < 6)
        norm = jnp.where(is_norm, norm, 0.0)
        ones = jnp.where(is_norm, 1.0, 0.0)
        source = jnp.concatenate([h + ones, m + norm, l, h, m, h] + [zero] * 10, axis=0)
        source_ref[columns, :] = source.T[:, :FEATURES].astype(bf16)
        if own:
            target = jnp.concatenate(
                [-2.0 * h + norm, -2.0 * h + ones, -2.0 * h, -2.0 * m, -2.0 * m, -2.0 * l], axis=0
            )
            target_ref[:, block(w - HALO_L, LEAF)] = target.astype(bf16)

    def own(b, carry):
        prepare(b + HALO_L, points_ref[:, block(b, LEAF)], True)
        return carry

    lax.fori_loop(0, LEAVES, own, 0, unroll=4)
    for i in range(HALO_L):
        columns = slice(i * LEAF, (i + 1) * LEAF)
        prepare(i, before_ref[:, columns], False)
        prepare(HALO_L + LEAVES + i, after_ref[:, columns], False)

    def leaf(a, carry):
        columns = block(a, LEAF)
        target = target_ref[:, columns]
        at = [block(list_ref[a, j], LEAF) for j in range(NEAR)]
        source = jnp.concatenate([source_ref[s, :] for s in at], axis=0)
        weight = jnp.concatenate([weight_ref[:, s] for s in at], axis=1)
        squared = jnp.dot(source, target, preferred_element_type=f32)
        parts = []
        for j in range(NEAR):
            r = jnp.maximum(squared[j * LEAF : (j + 1) * LEAF], FLOOR)
            t = r * lax.rsqrt(r)
            parts.append(jnp.concatenate(two((t + LOG2E) * jnp.exp2(-t)), axis=1))
        total = jnp.dot(weight, jnp.concatenate(parts, axis=0), preferred_element_type=f32)
        out_ref[:, columns] = total[:RHS, :LEAF] + total[RHS:, :LEAF] + total[:RHS, LEAF:]
        return carry

    lax.fori_loop(0, LEAVES, leaf, 0, unroll=4)


def weights_kernel(
    place_ref, coupling_in_ref, local_in_ref, group_ref, basis_ref,
    coupling_ref, wide_basis_ref, wide_ref, local_ref, path_in_ref, path_ref,
):
    spread_all(local_in_ref, local_ref, 2 * LEAVES - 2)
    spread_path(place_ref[0], group_ref, path_in_ref, path_ref)

    def leaf(a, carry):
        spread(coupling_in_ref[block(a, INTER), :], wide_ref, a * INTER)
        return carry

    lax.fori_loop(0, LEAVES, leaf, 0, unroll=2)

    def join(a, carry):
        joined = jnp.concatenate([matrix(wide_ref, a * INTER + j) for j in range(INTER)], axis=1)
        coupling_ref[a] = jnp.concatenate(two(joined), axis=0)
        return carry

    lax.fori_loop(0, LEAVES, join, 0, unroll=2)

    node = matrix(path_ref, 0)
    for i in range(1, PATH):
        node = dot(matrix(path_ref, i), node)
    nodes = [node]
    offset = 2 * LEAVES - 4
    while len(nodes) < LEAVES:
        nodes = [
            dot(node, matrix(local_ref, offset + 2 * i + k))
            for i, node in enumerate(nodes)
            for k in (0, 1)
        ]
        offset = offset - 2 * len(nodes)
    gain = DOWN ** (2 * PATH)
    for i, node in enumerate(nodes):
        columns = slice(i * LEAF, (i + 1) * LEAF)
        carried = gain * dot(node, basis_ref[:, columns])
        wide_basis_ref[:, columns] = jnp.concatenate(two(carried), axis=0)


def turned_parts(x):
    high = x.astype(bf16).astype(f32)
    stacked = jnp.concatenate([high, x - high, high, jnp.zeros_like(high)], axis=0)
    return stacked.T.astype(bf16)


def far_kernel(
    recv_ref, slots_ref, coupling_hbm, basis_hbm, wide_basis_hbm, near_hbm,
    out_hbm, coupling_ref, basis_ref, wide_basis_ref, near_ref, turned_ref,
    sems, out_sems,
):
    loads = [
        pltpu.make_async_copy(source, target, sems.at[i])
        for i, (source, target) in enumerate(
            (
                (coupling_hbm, coupling_ref),
                (basis_hbm, basis_ref),
                (wide_basis_hbm, wide_basis_ref),
                (near_hbm, near_ref),
            )
        )
    ]
    for load in loads:
        load.start()
    top = slots_ref[0, 4 * RANK :, :]
    for d in range(1, MEMBERS):
        top = top + slots_ref[d, 4 * RANK :, :]
    top = turned_parts(unfold(top))[:RHS]
    loads[0].wait()
    left = left_half((RANK, 2 * RHS))

    def far(a):
        picked = []
        for j in range(INTER):
            slot = recv_ref[0, a * INTER + j]
            use_left = (slot & 1) == 0
            rows = block(lax.shift_right_logical(slot, 1) & 3, RANK)
            picked.append(
                jnp.where(left == use_left, slots_ref[lax.shift_right_logical(slot, 3), rows, :], 0.0)
            )
        high, low = two(jnp.concatenate(picked, axis=0))
        y = jnp.dot(
            coupling_ref[a], jnp.concatenate([high, low], axis=1), preferred_element_type=f32
        )
        y = y[:RANK, : 2 * RHS] + y[:RANK, 2 * RHS :] + y[RANK:, : 2 * RHS]
        return y + swap(y)

    def turn(i, carry):
        turned_ref[i] = turned_parts(jnp.where(left, far(2 * i), far(2 * i + 1)))
        return carry

    lax.fori_loop(0, LEAVES // 2, turn, 0, unroll=8)
    for load in loads[1:]:
        load.wait()

    def finish(a, carry):
        columns = block(a, LEAF)
        basis_high, basis_low = two(basis_ref[:, columns])
        high, low = wide_basis_ref[:RANK, columns], wide_basis_ref[RANK:, columns]
        basis = jnp.concatenate(
            [basis_high, basis_high, basis_low, basis_low, high, high, low, low], axis=0
        )
        rows = turned_ref[lax.shift_right_logical(a, 1), block(a & 1, RHS), :]
        joined = jnp.concatenate([rows, top], axis=1)
        y = jnp.dot(joined, basis, preferred_element_type=f32)
        near_ref[:, columns] = near_ref[:, columns] + y
        return carry

    stores = []
    for i, part in enumerate(PARTS):
        lax.fori_loop(PART_L * i, PART_L * (i + 1), finish, 0, unroll=8)
        copy = pltpu.make_async_copy(near_ref.at[:, part], out_hbm.at[:, part], out_sems.at[i])
        copy.start()
        stores.append(copy)
    for copy in stores:
        copy.wait()


def call(kernel, name, outs, specs, scratch, kind=f32, out=vmem, aliases=None, limit=VMEM_BYTES):
    return pl.pallas_call(
        kernel,
        name=name,
        out_shape=[jax.ShapeDtypeStruct(s, kind) for s in outs],
        in_specs=specs,
        out_specs=[out] * len(outs),
        scratch_shapes=scratch,
        input_output_aliases=aliases or {},
        compiler_params=pltpu.CompilerParams(vmem_limit_bytes=limit),
        cost_estimate=pl.CostEstimate(flops=10**9, bytes_accessed=2**20, transcendentals=0),
    )


def shards(
    charges,
    coords,
    point_order,
    near_list,
    send_list,
    recv_list,
    leaf_basis,
    local_transfer,
    leaf_coupling,
    group_transfer,
    top_coupling,
):
    place = lax.axis_index("dev").astype(jnp.int32).reshape(1)
    wide = [
        pltpu.VMEM(((2 * LEAVES - 2) * RANK, LEAF), f32),
        pltpu.VMEM((8, RANK * RANK), f32),
        pltpu.VMEM((8 * RANK, LEAF), f32),
    ]
    points, first, last, coef, roots = call(
        order_kernel,
        "order",
        [
            (RHS + 8, PTS), (RHS + 8, HALO), (RHS + 8, HALO),
            (LEAVES, RANK, 2 * RHS), (GROUPS, RANK // 2, 2 * RHS),
        ],
        [smem, smem, hbm, vmem, hbm, hbm, hbm],
        [
            pltpu.VMEM((RHS, PTS), f32),
            pltpu.VMEM((RANK, PTS), f32),
            pltpu.VMEM((RHS + 8, PTS), f32),
            pltpu.VMEM((LEAVES, RANK, 2 * RHS), f32),
            pltpu.VMEM((PTS, LEAF), f32),
            pltpu.VMEM((PTS, LEAF), f32),
            pltpu.VMEM((8, PTS), f32),
            pltpu.VMEM((LEAVES // 2, RANK, 2 * RHS), f32),
            pltpu.VMEM((GROUPS, RANK // 2, 2 * RHS), f32),
            pltpu.VMEM((2 * LEAVES - 2, RANK * RANK), f32),
            pltpu.VMEM((2 * MEMBERS - 2, RANK * RANK), f32),
        ]
        + wide
        + [
            pltpu.SemaphoreType.DMA((len(PARTS) + 3,)),
            pltpu.SemaphoreType.DMA((2 * len(PARTS) + 3,)),
        ],
        out=hbm,
    )(place, point_order, charges, coords, leaf_basis, local_transfer, group_transfer)
    (sent,) = call(
        pack_kernel,
        "pack",
        [(MEMBERS, 4 * RANK + RANK // 2, 2 * RHS)],
        [smem, hbm],
        [
            pltpu.VMEM((LEAVES, RANK, 2 * RHS), f32),
            pltpu.VMEM((MEMBERS, 4 * RANK, 2 * RHS), f32),
            pltpu.SemaphoreType.DMA((5,)),
        ],
        out=hbm,
    )(send_list, coef)
    roots = lax.all_to_all(roots, "group", split_axis=0, concat_axis=0, tiled=True)
    size = lax.axis_size("group") * lax.axis_size("dev")
    up = [(i, i + 1) for i in range(size - 1)]
    back = [(i + 1, i) for i in range(size - 1)]
    before = lax.ppermute(last, ("group", "dev"), up)
    after = lax.ppermute(first, ("group", "dev"), back)
    roots, before, after = lax.optimization_barrier((roots, before, after))
    (sent,) = call(
        top_kernel,
        "top",
        [sent.shape],
        [vmem, vmem, hbm],
        [pltpu.VMEM((MEMBERS, RANK // 2, 2 * RHS), f32), pltpu.SemaphoreType.DMA],
        out=hbm,
        aliases={2: 0},
    )(roots, top_coupling, sent)
    slots = lax.all_to_all(sent, "dev", split_axis=0, concat_axis=0, tiled=True)
    (near,) = call(
        near_kernel,
        "near",
        [(RHS, PTS)],
        [smem, vmem, vmem, vmem],
        [
            pltpu.VMEM((FEATURES, PTS), bf16),
            pltpu.VMEM((WIN, FEATURES), bf16),
            pltpu.VMEM((2 * RHS, WIN), bf16),
        ],
        limit=LESS_VMEM,
    )(near_list, points, before, after)

    coupling, wide_basis = call(
        weights_kernel,
        "weights",
        [(LEAVES, 2 * RANK, INTER * RANK), (2 * RANK, PTS)],
        [smem] + [vmem] * 4,
        [pltpu.VMEM((LEAVES * INTER * RANK, LEAF), f32)] + wide,
        bf16,
        limit=LESS_VMEM,
    )(place, leaf_coupling, local_transfer, group_transfer, leaf_basis)
    (potential,) = call(
        far_kernel,
        "far",
        [(RHS, PTS)],
        [smem, vmem] + [hbm] * 4,
        [
            pltpu.VMEM((LEAVES, 2 * RANK, INTER * RANK), bf16),
            pltpu.VMEM((RANK, PTS), f32),
            pltpu.VMEM((2 * RANK, PTS), bf16),
            pltpu.VMEM((RHS, PTS), f32),
            pltpu.VMEM((LEAVES // 2, 2 * RHS, 2 * RHS), bf16),
            pltpu.SemaphoreType.DMA((4,)),
            pltpu.SemaphoreType.DMA((len(PARTS),)),
        ],
        out=hbm,
        limit=LESS_VMEM,
    )(recv_list, slots, coupling, leaf_basis, wide_basis, near)
    return potential


def solution(mesh):
    return jax.shard_map(
        shards,
        mesh=mesh,
        in_specs=(
            P(None, ("group", "dev")),
            P(None, ("group", "dev")),
            P(("group", "dev"), None),
            P(("group", "dev"), None),
            P(("group", "dev"), None),
            P(("group", "dev"), None),
            P(None, ("group", "dev")),
            P(("group", "dev"), None),
            P(("group", "dev"), None),
            P("group", None),
            P("group", None, None),
        ),
        out_specs=P(None, ("group", "dev")),
        check_vma=False,
    )
```
